32 devices in a mesh: dp: 4 (over y, x), ctx: 4 (over z), tensor: 2 (over core).
Axes of the slice: x: 2, y: 2, z: 4, core: 2. Of those that a mesh axis runs over, the one named last changes fastest.
Arguments:
- tokens: bfloat16 [8, 512, 1536], P('dp', ('ctx', 'tensor')), may hold values from -6 to 6
- prefix: int32 [8], P('dp'), may hold values from 51 to 256
- w_query: float32 [1536, 1536], P(('dp', 'ctx'), 'tensor'), may hold values from -0.15625 to 0.15625
- w_key: float32 [1536, 256], P(('dp', 'ctx'), 'tensor'), may hold values from -0.15625 to 0.15625
- w_value: float32 [1536, 256], P(('dp', 'ctx'), 'tensor'), may hold values from -0.15625 to 0.15625
- w_out: float32 [1536, 1536], P(('dp', 'ctx'), 'tensor'), may hold values from -0.5 to 0.5
- w_gate: float32 [1536, 8960], P(('dp', 'ctx'), 'tensor'), may hold values from -0.15625 to 0.15625
- w_up: float32 [1536, 8960], P(('dp', 'ctx'), 'tensor'), may hold values from -0.15625 to 0.15625
- w_down: float32 [1536, 8960], P(('dp', 'ctx'), 'tensor'), may hold values from -0.0625 to 0.0625
- b_query: float32 [1536], replicated, may hold values from -0.6 to 0.6
- b_key: float32 [256], replicated, may hold values from -1.5 to 1.5
- b_value: float32 [256], replicated, may hold values from -0.6 to 0.6
- norm_attn: float32 [1536], replicated, may hold values from 0.5 to 1.5
- norm_mlp: float32 [1536], replicated, may hold values from 0.5 to 1.5
- cotangent: bfloat16 [8, 512, 1536], P('dp', ('ctx', 'tensor')), may hold values from -6 to 6
Outputs:
- output: bfloat16 [8, 512, 1536], P('dp', ('ctx', 'tensor'))
- grad_tokens: bfloat16 [8, 512, 1536], P('dp', ('ctx', 'tensor'))
- grad_w_query: float32 [1536, 1536], P(('dp', 'ctx'), 'tensor')
- grad_w_key: float32 [1536, 256], P(('dp', 'ctx'), 'tensor')
- grad_w_value: float32 [1536, 256], P(('dp', 'ctx'), 'tensor')
- grad_w_out: float32 [1536, 1536], P(('dp', 'ctx'), 'tensor')
- grad_w_gate: float32 [1536, 8960], P(('dp', 'ctx'), 'tensor')
- grad_w_up: float32 [1536, 8960], P(('dp', 'ctx'), 'tensor')
- grad_w_down: float32 [1536, 8960], P(('dp', 'ctx'), 'tensor')
- grad_b_query: float32 [1536], replicated
- grad_b_key: float32 [256], replicated
- grad_b_value: float32 [256], replicated
- grad_norm_attn: float32 [1536], replicated
- grad_norm_mlp: float32 [1536], replicated
The draws below stay inside these ranges and needn't reach their ends.
All inputs are finite; a program needn't handle non-finite values.
Results may differ from the reference program's by a relative error of at most 0.029.
Values may be sent and summed in bfloat16 or wider, within the bound.
No kernel may reach another device: no remote copies, remote signals or barrier semaphores. Data moves between devices by JAX's collectives and lax.ppermute only.
A program may use at most 512 MiB of HBM per device.

```python
import jax
import jax.numpy as jnp
from jax import lax

D = 1536
H = 12
KV = 2
HD = 128
FF = 8960
SEQS = 8
LEN = 512


def set_ends(drawn, key, smallest, largest):
    spot = [jax.random.randint(jax.random.fold_in(key, axis), (), 0, length) for axis, length in enumerate(drawn.shape)]
    longest = drawn.shape.index(max(drawn.shape))
    beside = spot[:longest] + [(spot[longest] + 1) % drawn.shape[longest]] + spot[longest + 1:]
    return drawn.at[tuple(spot)].set(smallest).at[tuple(beside)].set(largest)


def shard_levels(stream_key, shape, shards, least, largest):
    level, own = 1.0, jax.random.fold_in(stream_key, 6)
    for position, shards_of in shards:
        draws = jnp.exp(jax.random.uniform(jax.random.fold_in(own, position), (shards_of,), jnp.float32, least / len(shards), largest / len(shards)))
        level = level * jnp.repeat(draws, shape[position] // shards_of).reshape([-1 if axis == position else 1 for axis in range(len(shape))])
    return level


def scatter_about(rng, dims, deviation, bound, cuts=(), kind=jnp.bfloat16):
    level = shard_levels(rng, dims, cuts, -0.22, 0.18) if cuts else 1.0
    entries = jax.random.normal(rng, dims, jnp.float32) * deviation * level
    return jnp.minimum(jnp.maximum(entries, -bound), bound).astype(kind)


def setup_inputs(seed: int = 0) -> dict:
    key_of = jax.random.split(jax.random.key(seed), 16)
    tokens = scatter_about(key_of[0], (SEQS, LEN, D), 1.0, 6.0, ((0, 4), (1, 8)))
    prefix = set_ends(jax.random.randint(key_of[1], (SEQS,), LEN // 10, LEN // 2 + 1), jax.random.fold_in(key_of[1], 1), LEN // 10, (LEN // 2 + 1) - 1).astype(jnp.int32)
    w_query = scatter_about(key_of[2], (D, H * HD), D ** -0.5, 0.15625, ((0, 16), (1, 2)), jnp.float32)
    w_key = scatter_about(key_of[3], (D, KV * HD), D ** -0.5, 0.15625, ((0, 16), (1, 2)), jnp.float32)
    w_value = scatter_about(key_of[4], (D, KV * HD), D ** -0.5, 0.15625, ((0, 16), (1, 2)), jnp.float32)
    w_out = scatter_about(key_of[5], (D, H * HD), HD ** -0.5, 0.5, ((0, 16), (1, 2)), jnp.float32)
    w_gate = scatter_about(key_of[6], (D, FF), D ** -0.5, 0.15625, ((0, 16), (1, 2)), jnp.float32)
    w_up = scatter_about(key_of[7], (D, FF), D ** -0.5, 0.15625, ((0, 16), (1, 2)), jnp.float32)
    w_down = scatter_about(key_of[8], (D, FF), FF ** -0.5, 0.0625, ((0, 16), (1, 2)), jnp.float32)
    b_query = scatter_about(key_of[9], (H * HD,), 0.1, 0.6, (), jnp.float32)
    b_key = scatter_about(key_of[10], (KV * HD,), 0.25, 1.5, (), jnp.float32)
    b_value = scatter_about(key_of[11], (KV * HD,), 0.1, 0.6, (), jnp.float32)
    norm_attn = jnp.clip(1.0 + 0.1 * jax.random.normal(key_of[12], (D,), jnp.float32), 0.5, 1.5)
    norm_mlp = jnp.clip(1.0 + 0.1 * jax.random.normal(key_of[13], (D,), jnp.float32), 0.5, 1.5)
    cotangent = scatter_about(key_of[14], (SEQS, LEN, D), 1.0, 6.0, ((0, 4), (1, 8)))
    return {"tokens": tokens, "prefix": prefix, "w_query": w_query, "w_key": w_key, "w_value": w_value, "w_out": w_out, "w_gate": w_gate, "w_up": w_up, "w_down": w_down, "b_query": b_query, "b_key": b_key, "b_value": b_value, "norm_attn": norm_attn, "norm_mlp": norm_mlp, "cotangent": cotangent}


epsilon = 1e-06
rope_base = 1000000.0
highest = lax.Precision.HIGHEST

@jax.custom_vjp
def low(v):
    return lax.optimization_barrier(v.astype(jnp.bfloat16)).astype(jnp.float32)

@jax.custom_vjp
def low_back(v):
    return v

def low_keep(v):
    return (low(v), None)

def low_pass(kept, grad):
    return (grad,)

def back_keep(v):
    return (v, None)

def back_low(kept, grad):
    return (low(grad),)
low.defvjp(low_keep, low_pass)
low_back.defvjp(back_keep, back_low)

def inverse_root(value):
    return lax.rsqrt(lax.optimization_barrier(jnp.mean(value * value, axis=-1, keepdims=True)) + epsilon)

def rotary_tables(positions):
    half_dim = HD // 2
    frequency = rope_base ** (-2.0 * jnp.arange(half_dim, dtype=jnp.float32) / HD)
    angles = positions.astype(jnp.float32)[:, None] * frequency[None, :]
    angles = jnp.concatenate([angles, angles], axis=1)
    return (jnp.cos(angles)[:, None, :], jnp.sin(angles)[:, None, :])

def rotate(value, cosine_table, sine_table):
    half_dim = value.shape[-1] // 2
    turned = jnp.concatenate([-value[..., half_dim:], value[..., :half_dim]], axis=-1)
    return value * cosine_table + turned * sine_table

def matmul(left, right):
    return jnp.dot(left, right, precision=highest, preferred_element_type=jnp.float32)

def block_forward(seq_tokens, prefix_len, weights):
    w_query, w_key, w_value, w_out, w_gate, w_up, w_down, b_query, b_key, b_value, norm_attn, norm_mlp = weights
    qblock = min(512, LEN)
    attn_root = inverse_root(seq_tokens)
    normed1 = low(seq_tokens * attn_root * norm_attn)
    query_pre = low_back(matmul(normed1, low(w_query)) + b_query)
    key_pre = low_back(matmul(normed1, low(w_key)) + b_key)
    value_rows = low(low_back(matmul(normed1, low(w_value)) + b_value)).reshape(LEN, KV, HD)
    positions = jnp.arange(LEN, dtype=jnp.int32)
    cosine_table, sine_table = rotary_tables(positions)
    queries = low(rotate(query_pre.reshape(LEN, H, HD), cosine_table, sine_table))
    queries = queries.reshape(LEN // qblock, qblock, KV, H // KV, HD)
    key_rows = low(rotate(key_pre.reshape(LEN, KV, HD), cosine_table, sine_table))
    score_scale = HD ** (-0.5)

    def query_block(block_args):
        query_rows, query_pos = block_args
        raw_scores = low_back(jnp.einsum('cahd,lad->ahcl', query_rows, key_rows, precision=highest) * score_scale)
        allowed = (positions[None, :] <= query_pos[:, None]) | (positions[None, :] < prefix_len)
        masked = jnp.where(allowed[None, None], raw_scores, -1e+30)
        soft = jax.nn.softmax(masked, axis=-1)
        return jnp.einsum('ahcl,lad->cahd', low(soft), value_rows, precision=highest)
    mixed_heads = lax.map(jax.checkpoint(query_block), (queries, positions.reshape(LEN // qblock, qblock)))
    mixed_low = low(low_back(mixed_heads.reshape(LEN, H * HD)))
    hidden1 = seq_tokens + low_back(matmul(mixed_low, low(w_out).T))
    mlp_root = inverse_root(hidden1)
    normed2 = low(hidden1 * mlp_root * norm_mlp)
    gate_pre = low_back(matmul(normed2, low(w_gate)))
    up_pre = low_back(matmul(normed2, low(w_up)))
    activation = low(jax.nn.silu(gate_pre) * up_pre)
    return hidden1 + low_back(matmul(activation, low(w_down).T))

def reference(tokens, prefix, w_query, w_key, w_value, w_out, w_gate, w_up, w_down, b_query, b_key, b_value, norm_attn, norm_mlp, cotangent):
    params = (w_query, w_key, w_value, w_out, w_gate, w_up, w_down, b_query, b_key, b_value, norm_attn, norm_mlp)

    def per_sequence(carry, seq_item):
        seq_tokens, seq_cotangent, prefix_len = seq_item

        def forward(inputs, weights):
            return block_forward(inputs, prefix_len, weights)
        result, pullback = jax.vjp(forward, seq_tokens.astype(jnp.float32), params)
        grad_inputs, grad_params = pullback(seq_cotangent.astype(jnp.float32))
        updated = tuple((summed + extra for summed, extra in zip(carry, grad_params)))
        return (updated, (result.astype(jnp.bfloat16), grad_inputs.astype(jnp.bfloat16)))
    start_sums = tuple((jnp.zeros_like(param) for param in params))
    totals, (outputs, grad_tokens) = lax.scan(per_sequence, start_sums, (tokens, cotangent, prefix))
    return (outputs, grad_tokens, totals[0], totals[1], totals[2], totals[3], totals[4], totals[5], totals[6], totals[7], totals[8], totals[9], totals[10], totals[11])
```

```python
import jax
import jax.numpy as jnp
from jax import lax
from jax.sharding import PartitionSpec as P

HD = 128


epsilon = 1e-06
rope_base = 1000000.0


def inverse_root(value):
    return lax.rsqrt(jnp.mean(value * value, axis=-1, keepdims=True) + epsilon)


def rotary_tables(positions):
    half_dim = HD // 2
    frequency = rope_base ** (-2.0 * jnp.arange(half_dim, dtype=jnp.float32) / HD)
    angles = positions.astype(jnp.float32)[:, None] * frequency[None, :]
    angles = jnp.concatenate([angles, angles], axis=1)
    return (jnp.cos(angles)[:, None, :], jnp.sin(angles)[:, None, :])


def rotate(value, cosine_table, sine_table):
    half_dim = value.shape[-1] // 2
    turned = jnp.concatenate([-value[..., half_dim:], value[..., :half_dim]], axis=-1)
    return value * cosine_table + turned * sine_table


def rotate_back(grad_rows, cosine_table, sine_table):
    half_dim = grad_rows.shape[-1] // 2
    scaled = grad_rows * sine_table
    turned = jnp.concatenate([scaled[..., half_dim:], -scaled[..., :half_dim]], axis=-1)
    return grad_rows * cosine_table + turned


def scores_of(queries, key_rows, allowed, score_scale):
    raw_scores = (
        jnp.einsum("cahd,lad->ahcl", queries, key_rows, preferred_element_type=jnp.float32)
        * score_scale
    )
    return jnp.where(allowed[None, None], raw_scores, -1e30)


def attend(queries, key_rows, values, allowed, score_scale):
    scores = scores_of(queries, key_rows, allowed, score_scale)
    peak = jnp.max(scores, axis=-1, keepdims=True)
    weights = jnp.exp(scores - peak)
    denominator = jnp.sum(weights, axis=-1, keepdims=True)
    probabilities = (weights / denominator).astype(jnp.bfloat16)
    mixed_heads = jnp.einsum(
        "ahcl,lad->cahd", probabilities, values, preferred_element_type=jnp.float32
    )
    return (mixed_heads, peak + jnp.log(denominator))


def attend_back(
    queries, key_rows, values, allowed, score_scale, log_total, mixed_heads, grad_mixed
):
    scores = scores_of(queries, key_rows, allowed, score_scale)
    probabilities = jnp.exp(scores - log_total)
    grad_probs = jnp.einsum(
        "cahd,lad->ahcl", grad_mixed, values, preferred_element_type=jnp.float32
    )
    offset = jnp.einsum("cahd,cahd->ahc", grad_mixed.astype(jnp.float32), mixed_heads)[..., None]
    grad_scores = (probabilities * (grad_probs - offset)).astype(jnp.bfloat16)
    grad_query = (
        jnp.einsum("ahcl,lad->cahd", grad_scores, key_rows, preferred_element_type=jnp.float32)
        * score_scale
    )
    grad_key = (
        jnp.einsum("ahcl,cahd->lad", grad_scores, queries, preferred_element_type=jnp.float32)
        * score_scale
    )
    grad_value = jnp.einsum(
        "ahcl,cahd->lad",
        probabilities.astype(jnp.bfloat16),
        grad_mixed,
        preferred_element_type=jnp.float32,
    )
    return (grad_query, grad_key, grad_value)


def project_back(left, right):
    return jnp.einsum("rf,df->rd", left, right, preferred_element_type=jnp.float32)


def weight_term(left, right):
    return jnp.einsum("rd,rc->dc", left, right, preferred_element_type=jnp.float32)


def update_at(target, block, index):
    return lax.dynamic_update_index_in_dim(target, block, index, 0)


def pick(source, index, axis=0):
    return lax.dynamic_index_in_dim(source, index, axis, keepdims=False)


def swap_tensor(value):
    return lax.ppermute(value, "tensor", [(0, 1), (1, 0)])


def shift_ctx(value, distance):
    size = lax.axis_size("ctx")
    return lax.ppermute(value, "ctx", [(i, (i + distance) % size) for i in range(size)])


def swap_dp(value, bit):
    return lax.ppermute(value, "dp", [(i, i ^ bit) for i in range(lax.axis_size("dp"))])


def ring_blocks(value):
    blocks = [value]
    for _ in range(lax.axis_size("ctx") - 1):
        blocks.append(shift_ctx(blocks[-1], 1))
    return blocks


def ring_sum(blocks):
    size = lax.axis_size("ctx")
    total = blocks[1 % size]
    for step in range(1, size):
        total = shift_ctx(total.astype(jnp.bfloat16), 1).astype(jnp.float32)
        total = total + blocks[(step + 1) % size].astype(jnp.float32)
    return total


def spread_ctx(columns):
    size = lax.axis_size("ctx")
    own = lax.axis_index("ctx")
    gathered = jnp.zeros_like(columns)
    gathered = update_at(gathered, pick(columns, own), own)
    for distance in range(1, size):
        got = shift_ctx(pick(columns, (own + distance) % size), distance)
        gathered = update_at(gathered, got, (own - distance) % size)
    return gathered


def gather_ctx(value):
    size = lax.axis_size("ctx")
    own = lax.axis_index("ctx")
    gathered = jnp.zeros((size,) + value.shape, value.dtype)
    for distance, block in enumerate(ring_blocks(value)):
        gathered = update_at(gathered, block, (own - distance) % size)
    return gathered


def gather_dp(value):
    rows, columns = value.shape
    own = lax.axis_index("dp")
    low, high = own % 2, own // 2
    half = rows // 2
    first, second = value[:half], value[half:]
    full = jnp.zeros((2, 2, 2, half, columns), value.dtype)
    pair_x = jnp.zeros((2, half, columns), value.dtype)
    pair_x = update_at(update_at(pair_x, first, low), swap_dp(first, 1), 1 - low)
    pair_y = jnp.zeros((2, half, columns), value.dtype)
    pair_y = update_at(update_at(pair_y, second, high), swap_dp(second, 2), 1 - high)
    far_x = swap_dp(pair_x, 2)
    far_y = swap_dp(pair_y, 1)
    full = lax.dynamic_update_slice(full, pair_x[None, :, None], (high, 0, 0, 0, 0))
    full = lax.dynamic_update_slice(full, far_x[None, :, None], (1 - high, 0, 0, 0, 0))
    full = lax.dynamic_update_slice(full, pair_y[:, None, None], (0, low, 1, 0, 0))
    full = lax.dynamic_update_slice(full, far_y[:, None, None], (0, 1 - low, 1, 0, 0))
    return full.reshape(4 * rows, columns)


def scatter_dp(value):
    rows, columns = value.shape[0] // 4, value.shape[1]
    own = lax.axis_index("dp")
    low, high = own % 2, own // 2
    half = rows // 2
    terms = value.reshape(2, 2, 2, half, columns)
    first, second = terms[:, :, 0], terms[:, :, 1]
    sent_x = swap_dp(pick(first, 1 - low, 1).astype(jnp.bfloat16), 1)
    sent_y = swap_dp(pick(second, 1 - high, 0).astype(jnp.bfloat16), 2)
    pair_x = pick(first, low, 1).astype(jnp.float32) + sent_x.astype(jnp.float32)
    pair_y = pick(second, high, 0).astype(jnp.float32) + sent_y.astype(jnp.float32)
    last_x = swap_dp(pick(pair_x, 1 - high).astype(jnp.bfloat16), 2)
    last_y = swap_dp(pick(pair_y, 1 - low).astype(jnp.bfloat16), 1)
    return jnp.concatenate(
        [
            pick(pair_x, high) + last_x.astype(jnp.float32),
            pick(pair_y, low) + last_y.astype(jnp.float32),
        ],
        axis=0,
    )


def hidden_weight(weight, ff_part):
    rows, columns = weight.shape
    size = lax.axis_size("ctx")
    wide = jnp.pad(weight.astype(jnp.bfloat16), ((0, 0), (0, size * ff_part - columns)))
    parts = jnp.stack([wide[:, c * ff_part : (c + 1) * ff_part] for c in range(size)])
    return gather_dp(spread_ctx(parts).reshape(size * rows, ff_part))


def hidden_grad(term, columns):
    size = lax.axis_size("ctx")
    mine = scatter_dp(term).astype(jnp.bfloat16)
    ff_part = mine.shape[1]
    parts = spread_ctx(mine.reshape(size, -1, ff_part))
    wide = jnp.concatenate([parts[c] for c in range(size)], axis=1)
    return wide[:, :columns].astype(jnp.float32)


def attn_grad(term):
    size = lax.axis_size("ctx")
    own = lax.axis_index("ctx")
    mine = scatter_dp(term)
    parts = mine.reshape(size, -1, mine.shape[1])
    return ring_sum([pick(parts, (own - j) % size) for j in range(size)])


def gather_span(value):
    mine = jnp.concatenate([b.reshape(-1, b.shape[-1]) for b in ring_blocks(value)], axis=0)
    return jnp.concatenate([mine, swap_tensor(mine)], axis=0)


def scatter_span(term, shape):
    size = lax.axis_size("ctx")
    half = term.shape[0] // 2
    mine = term[:half].astype(jnp.float32) + swap_tensor(term[half:].astype(jnp.bfloat16)).astype(
        jnp.float32
    )
    blocks = mine.reshape(size, half // size, -1)
    return ring_sum([blocks[j] for j in range(size)]).reshape(shape)


def per_device(
    tokens,
    prefix,
    w_query,
    w_key,
    w_value,
    w_out,
    w_gate,
    w_up,
    w_down,
    b_query,
    b_key,
    b_value,
    norm_attn,
    norm_mlp,
    cotangent,
):
    bf16, f32 = jnp.bfloat16, jnp.float32
    seq_dev, own_rows, model_width = tokens.shape
    ctx_size = lax.axis_size("ctx")
    span_len = own_rows * 2
    seq_len = span_len * ctx_size
    row_count = seq_dev * span_len
    q_cols = w_query.shape[1]
    kv_cols = w_key.shape[1]
    ff_cols = w_gate.shape[1]
    ff_part = -(-ff_cols // (128 * ctx_size)) * 128
    kv_heads = kv_cols // HD
    group_size = q_cols // kv_cols
    score_scale = HD ** (-0.5)
    tensor_at = lax.axis_index("tensor")
    ctx_at = lax.axis_index("ctx")
    own_pos = jnp.arange(own_rows, dtype=jnp.int32)
    in_span = jnp.concatenate([tensor_at * own_rows + own_pos, (1 - tensor_at) * own_rows + own_pos])
    local_pos = ctx_at * span_len + in_span
    key_pos = jnp.concatenate(
        [((ctx_at - j) % ctx_size) * span_len + in_span for j in range(ctx_size)]
    )
    cosine_table, sine_table = rotary_tables(local_pos)
    bias_query = lax.dynamic_slice_in_dim(b_query, tensor_at * q_cols, q_cols)
    bias_key = lax.dynamic_slice_in_dim(b_key, tensor_at * kv_cols, kv_cols)
    bias_value = lax.dynamic_slice_in_dim(b_value, tensor_at * kv_cols, kv_cols)
    bias_all = jnp.concatenate([bias_query, bias_key, bias_value])
    cast_qkv = jnp.concatenate([w.astype(bf16) for w in (w_query, w_key, w_value)], axis=1)
    full_qkv = gather_dp(gather_ctx(cast_qkv).reshape(-1, cast_qkv.shape[1]))
    full_out = gather_dp(gather_ctx(w_out.astype(bf16)).reshape(-1, q_cols))
    full_gate = hidden_weight(w_gate, ff_part)
    full_up = hidden_weight(w_up, ff_part)
    full_down = hidden_weight(w_down, ff_part)

    x_own = tokens.astype(f32)
    attn_root = inverse_root(x_own)
    normed_own = (x_own * attn_root * norm_attn).astype(bf16)
    normed1 = jnp.concatenate([normed_own, swap_tensor(normed_own)], axis=1).reshape(
        row_count, model_width
    )
    qkv_pre = jnp.dot(normed1, full_qkv, preferred_element_type=f32) + bias_all
    query_pre = qkv_pre[:, :q_cols]
    key_pre = qkv_pre[:, q_cols : q_cols + kv_cols]
    value_pre = qkv_pre[:, q_cols + kv_cols :]
    queries = rotate(
        query_pre.reshape(seq_dev, span_len, q_cols // HD, HD), cosine_table, sine_table
    ).astype(bf16)
    queries = queries.reshape(seq_dev, span_len, kv_heads, group_size, HD)
    keys_own = rotate(
        key_pre.reshape(seq_dev, span_len, kv_heads, HD), cosine_table, sine_table
    ).astype(bf16)
    values_own = value_pre.reshape(seq_dev, span_len, kv_heads, HD).astype(bf16)
    both = jnp.concatenate(ring_blocks(jnp.stack([keys_own, values_own])), axis=2)
    key_rows, value_rows = both[0], both[1]
    masks = []
    mixed_list = []
    log_totals = []
    for seq_index in range(seq_dev):
        allowed = (key_pos[None, :] <= local_pos[:, None]) | (key_pos[None, :] < prefix[seq_index])
        mixed_heads, log_total = attend(
            queries[seq_index], key_rows[seq_index], value_rows[seq_index], allowed, score_scale
        )
        masks.append(allowed)
        mixed_list.append(mixed_heads)
        log_totals.append(log_total)
    mixed_full = jnp.stack(mixed_list)
    mixed_low = mixed_full.reshape(row_count, q_cols).astype(bf16)
    attn_term = project_back(mixed_low, full_out).reshape(seq_dev, span_len, model_width)
    hidden1 = (
        x_own
        + attn_term[:, :own_rows]
        + swap_tensor(attn_term[:, own_rows:].astype(bf16)).astype(f32)
    )
    mlp_root = inverse_root(hidden1)
    normed2 = gather_span((hidden1 * mlp_root * norm_mlp).astype(bf16))
    grad_mlp = gather_span(cotangent)
    gate_pre = jnp.dot(normed2, full_gate, preferred_element_type=f32)
    up_pre = jnp.dot(normed2, full_up, preferred_element_type=f32)
    sigmoid_gate = jax.nn.sigmoid(gate_pre)
    activation = (gate_pre * sigmoid_gate * up_pre).astype(bf16)
    grad_w_down = hidden_grad(weight_term(grad_mlp, activation), ff_cols)
    grad_act = jnp.dot(grad_mlp, full_down, preferred_element_type=f32)
    grad_up = (grad_act * gate_pre * sigmoid_gate).astype(bf16)
    grad_gate = (grad_act * up_pre * sigmoid_gate * (1.0 + gate_pre * (1.0 - sigmoid_gate))).astype(
        bf16
    )
    mlp_back = project_back(grad_gate, full_gate) + project_back(grad_up, full_up)
    grad_normed2 = scatter_span(mlp_back, tokens.shape)
    grad_w_gate = hidden_grad(weight_term(normed2, grad_gate), ff_cols)
    grad_w_up = hidden_grad(weight_term(normed2, grad_up), ff_cols)
    mlp_term = project_back(activation, full_down)
    output = (hidden1 + scatter_span(mlp_term, tokens.shape)).astype(bf16)
    grad_out = cotangent.astype(f32)
    scaled2 = norm_mlp * grad_normed2
    grad_hidden1 = (
        grad_out
        + mlp_root * scaled2
        - hidden1 * mlp_root**3 * jnp.mean(scaled2 * hidden1, axis=-1, keepdims=True)
    )
    gain_mlp = jnp.sum(grad_normed2 * hidden1 * mlp_root, axis=(0, 1))
    grad_own = grad_hidden1.astype(bf16)
    grad_attn = jnp.concatenate([grad_own, swap_tensor(grad_own)], axis=1).reshape(
        row_count, model_width
    )
    grad_w_out = attn_grad(weight_term(grad_attn, mixed_low))
    grad_mixed = jnp.dot(grad_attn, full_out, preferred_element_type=f32).astype(bf16)
    grad_mixed = grad_mixed.reshape(seq_dev, span_len, kv_heads, group_size, HD)
    query_grads = []
    key_grads = []
    value_grads = []
    for seq_index in range(seq_dev):
        grad_query, grad_key, grad_value = attend_back(
            queries[seq_index],
            key_rows[seq_index],
            value_rows[seq_index],
            masks[seq_index],
            score_scale,
            log_totals[seq_index],
            mixed_list[seq_index],
            grad_mixed[seq_index],
        )
        query_grads.append(grad_query)
        key_grads.append(grad_key)
        value_grads.append(grad_value)
    kv_terms = jnp.stack([jnp.stack(key_grads), jnp.stack(value_grads)])
    kv_sum = ring_sum(
        [kv_terms[:, :, j * span_len : (j + 1) * span_len] for j in range(ctx_size)]
    )
    grad_q = rotate_back(
        jnp.stack(query_grads).reshape(seq_dev, span_len, q_cols // HD, HD),
        cosine_table,
        sine_table,
    )
    grad_q = grad_q.reshape(row_count, q_cols).astype(bf16)
    grad_k = rotate_back(kv_sum[0], cosine_table, sine_table).reshape(row_count, kv_cols)
    grad_k = grad_k.astype(bf16)
    grad_v = kv_sum[1].reshape(row_count, kv_cols).astype(bf16)
    grad_qkv = jnp.concatenate([grad_q, grad_k, grad_v], axis=1)
    attn_back = project_back(grad_qkv, full_qkv).reshape(seq_dev, span_len, model_width)
    grad_w_qkv = attn_grad(weight_term(normed1, grad_qkv))
    grad_normed1 = attn_back[:, :own_rows] + swap_tensor(
        attn_back[:, own_rows:].astype(bf16)
    ).astype(f32)
    scaled1 = norm_attn * grad_normed1
    grad_tokens = (
        grad_hidden1
        + attn_root * scaled1
        - x_own * attn_root**3 * jnp.mean(scaled1 * x_own, axis=-1, keepdims=True)
    ).astype(bf16)
    gain_attn = jnp.sum(grad_normed1 * x_own * attn_root, axis=(0, 1))
    place_query = lax.dynamic_update_slice_in_dim(
        jnp.zeros_like(b_query), jnp.sum(grad_q, axis=0, dtype=f32), tensor_at * q_cols, 0
    )
    place_key = lax.dynamic_update_slice_in_dim(
        jnp.zeros_like(b_key), jnp.sum(grad_k, axis=0, dtype=f32), tensor_at * kv_cols, 0
    )
    place_value = lax.dynamic_update_slice_in_dim(
        jnp.zeros_like(b_value), jnp.sum(grad_v, axis=0, dtype=f32), tensor_at * kv_cols, 0
    )
    sum_attn, sum_mlp, sum_query, sum_key, sum_value = lax.psum(
        (gain_attn, gain_mlp, place_query, place_key, place_value), ("dp", "ctx", "tensor")
    )
    grad_w_query = grad_w_qkv[:, :q_cols]
    grad_w_key = grad_w_qkv[:, q_cols : q_cols + kv_cols]
    grad_w_value = grad_w_qkv[:, q_cols + kv_cols :]
    return (
        output,
        grad_tokens,
        grad_w_query,
        grad_w_key,
        grad_w_value,
        grad_w_out,
        grad_w_gate,
        grad_w_up,
        grad_w_down,
        sum_query,
        sum_key,
        sum_value,
        sum_attn,
        sum_mlp,
    )


def solution(mesh):
    placed = (
        P("dp", ("ctx", "tensor"), None),
        P("dp"),
        P(("dp", "ctx"), "tensor"),
        P(("dp", "ctx"), "tensor"),
        P(("dp", "ctx"), "tensor"),
        P(("dp", "ctx"), "tensor"),
        P(("dp", "ctx"), "tensor"),
        P(("dp", "ctx"), "tensor"),
        P(("dp", "ctx"), "tensor"),
        P(),
        P(),
        P(),
        P(),
        P(),
        P("dp", ("ctx", "tensor"), None),
    )
    return jax.shard_map(
        per_device,
        mesh=mesh,
        in_specs=placed,
        out_specs=(
            P("dp", ("ctx", "tensor"), None),
            P("dp", ("ctx", "tensor"), None),
            P(("dp", "ctx"), "tensor"),
            P(("dp", "ctx"), "tensor"),
            P(("dp", "ctx"), "tensor"),
            P(("dp", "ctx"), "tensor"),
            P(("dp", "ctx"), "tensor"),
            P(("dp", "ctx"), "tensor"),
            P(("dp", "ctx"), "tensor"),
            P(),
            P(),
            P(),
            P(),
            P(),
        ),
        check_vma=False,
    )
```

```python
import functools

import jax
import jax.numpy as jnp
from jax import lax
from jax.experimental import pallas as pl
from jax.experimental.pallas import tpu as pltpu
from jax.sharding import PartitionSpec as P

HD = 128


epsilon = 1e-06
rope_base = 1000000.0


def inverse_root(value):
    return lax.rsqrt(jnp.mean(value * value, axis=-1, keepdims=True) + epsilon)


def rotary_tables(positions):
    half_dim = HD // 2
    frequency = rope_base ** (-2.0 * jnp.arange(half_dim, dtype=jnp.float32) / HD)
    angles = positions.astype(jnp.float32)[:, None] * frequency[None, :]
    angles = jnp.concatenate([angles, angles], axis=1)
    return (jnp.cos(angles)[:, None, :], jnp.sin(angles)[:, None, :])


VMEM_LIMIT = 44 * 1024 * 1024


def params():
    return pltpu.CompilerParams(vmem_limit_bytes=VMEM_LIMIT)


def cost(flops, arrays):
    moved = sum(a.size * a.dtype.itemsize for a in arrays)
    return pl.CostEstimate(flops=flops, bytes_accessed=moved, transcendentals=0)


def contract(left, right, dims):
    return lax.dot_general(left, right, (dims, ((), ())), preferred_element_type=jnp.float32)


def half_sign(shape):
    return jnp.where(lax.broadcasted_iota(jnp.int32, shape, 1) < shape[1] // 2, 1.0, -1.0)


def qkv_kernel(rope_heads, x_ref, w_ref, b_ref, cos_ref, sin_ref, out_ref):
    at = pl.program_id(0)
    heads = w_ref.shape[1] // HD
    total = contract(x_ref[...], w_ref[...], ((1,), (0,))) + b_ref[...]
    cosine, sine = cos_ref[...], sin_ref[...]
    signed = -half_sign(sine.shape) * sine
    for head in range(heads):
        value = total[:, head * HD : (head + 1) * HD]
        turned = value * cosine + pltpu.roll(value, HD // 2, 1) * signed
        kept = jnp.where(at * heads + head < rope_heads, turned, value)
        out_ref[:, head * HD : (head + 1) * HD] = kept.astype(out_ref.dtype)


def qkv_heads(x, weight, bias, cosine, sine, rope_heads):
    rows, columns = x.shape[0], weight.shape[1]
    out = jax.ShapeDtypeStruct((rows, columns), jnp.bfloat16)
    whole = lambda a: pl.BlockSpec(a.shape, lambda i: (0, 0))
    return pl.pallas_call(
        functools.partial(qkv_kernel, rope_heads),
        out_shape=out,
        grid=(columns // 256,),
        in_specs=[
            whole(x),
            pl.BlockSpec((weight.shape[0], 256), lambda i: (0, i)),
            pl.BlockSpec((1, 256), lambda i: (0, i)),
            whole(cosine),
            whole(sine),
        ],
        out_specs=pl.BlockSpec((rows, 256), lambda i: (0, i)),
        compiler_params=params(),
        cost_estimate=cost(2 * x.size * columns, [x, weight, out]),
        name="qkv_heads",
    )(x, weight, bias, cosine, sine)


def probabilities_of(query, keys, allowed):
    scores = contract(query, keys, ((1,), (1,))) * HD ** (-0.5)
    scores = jnp.where(allowed, scores, -1e30)
    weights = jnp.exp(scores - jnp.max(scores, axis=-1, keepdims=True))
    return weights / jnp.sum(weights, axis=-1, keepdims=True)


def allowed_of(prefix_ref, row_ref, key_ref):
    keys = key_ref[...]
    return (keys <= row_ref[...]) | (keys < prefix_ref[pl.program_id(0)])


def attend_kernel(prefix_ref, row_ref, key_ref, q_ref, kv_ref, out_ref):
    allowed = allowed_of(prefix_ref, row_ref, key_ref)
    keys, values = kv_ref[0, :, :HD], kv_ref[0, :, HD:]
    for head in range(q_ref.shape[1] // HD):
        columns = slice(head * HD, (head + 1) * HD)
        chances = probabilities_of(q_ref[:, columns], keys, allowed).astype(jnp.bfloat16)
        out_ref[:, columns] = contract(chances, values, ((1,), (0,))).astype(out_ref.dtype)


def attend_back_kernel(
    prefix_ref, row_ref, key_ref, q_ref, kv_ref, grad_ref, cos_ref, sin_ref, dq_ref, dkv_ref
):
    allowed = allowed_of(prefix_ref, row_ref, key_ref)
    keys, values = kv_ref[0, :, :HD], kv_ref[0, :, HD:]
    sign = half_sign(cos_ref.shape)
    scale = HD ** (-0.5)
    grad_keys = jnp.zeros(keys.shape, jnp.float32)
    grad_values = jnp.zeros(keys.shape, jnp.float32)
    for head in range(q_ref.shape[1] // HD):
        columns = slice(head * HD, (head + 1) * HD)
        query, grad = q_ref[:, columns], grad_ref[:, columns]
        chances = probabilities_of(query, keys, allowed)
        rounded = chances.astype(jnp.bfloat16)
        grad_chances = contract(grad, values, ((1,), (1,)))
        offset = jnp.sum(rounded.astype(jnp.float32) * grad_chances, axis=-1, keepdims=True)
        grad_scores = (chances * (grad_chances - offset)).astype(jnp.bfloat16)
        turned = contract(grad_scores, keys, ((1,), (0,))) * scale
        back = turned * cos_ref[...] + pltpu.roll(turned * sin_ref[...], HD // 2, 1) * sign
        dq_ref[:, columns] = back.astype(dq_ref.dtype)
        grad_keys += contract(grad_scores, query, ((0,), (0,)))
        grad_values += contract(rounded, grad, ((0,), (0,)))
    dkv_ref[0, :, :HD] = (grad_keys * scale).astype(dkv_ref.dtype)
    dkv_ref[0, :, HD:] = grad_values.astype(dkv_ref.dtype)


def attention_specs(query, kv, row_pos, key_pos):
    rows = query.shape[0] // kv.shape[0]
    heads = pl.BlockSpec((rows, query.shape[1]), lambda i: (i, 0))
    both = pl.BlockSpec((1,) + kv.shape[1:], lambda i: (i, 0, 0))
    return heads, [
        pl.BlockSpec(memory_space=pltpu.SMEM),
        pl.BlockSpec(row_pos.shape, lambda i: (0, 0)),
        pl.BlockSpec(key_pos.shape, lambda i: (0, 0)),
        heads,
        both,
    ], both


def attend(prefix, row_pos, key_pos, query, kv):
    heads, specs, _ = attention_specs(query, kv, row_pos, key_pos)
    return pl.pallas_call(
        attend_kernel,
        out_shape=jax.ShapeDtypeStruct(query.shape, jnp.bfloat16),
        grid=(kv.shape[0],),
        in_specs=specs,
        out_specs=heads,
        compiler_params=params(),
        cost_estimate=cost(4 * query.size * kv.shape[1], [query, kv, query]),
        name="attend",
    )(prefix, row_pos, key_pos, query, kv)


def attend_back(prefix, row_pos, key_pos, query, kv, grad, cosine, sine):
    heads, specs, both = attention_specs(query, kv, row_pos, key_pos)
    table = pl.BlockSpec(cosine.shape, lambda i: (0, 0))
    return pl.pallas_call(
        attend_back_kernel,
        out_shape=(
            jax.ShapeDtypeStruct(query.shape, jnp.bfloat16),
            jax.ShapeDtypeStruct(kv.shape, jnp.bfloat16),
        ),
        grid=(kv.shape[0],),
        in_specs=specs + [heads, table, table],
        out_specs=(heads, both),
        compiler_params=params(),
        cost_estimate=cost(10 * query.size * kv.shape[1], [query, kv, grad, query, kv]),
        name="attend_back",
    )(prefix, row_pos, key_pos, query, kv, grad, cosine, sine)


STEP = 384
ROWS = 1024


def whole_block(array):
    return pl.BlockSpec(array.shape, lambda i: (0, 0))


def column_block(array, columns):
    return pl.BlockSpec((array.shape[0], columns), lambda i: (0, i))


def row_block(array, rows):
    return pl.BlockSpec((rows, array.shape[1]), lambda i: (i, 0))


def hidden_kernel(x_ref, gate_ref, up_ref, act_ref, silu_ref, slope_ref):
    x = x_ref[...]
    gate = contract(x, gate_ref[...], ((1,), (0,)))
    up = contract(x, up_ref[...], ((1,), (0,)))
    sigmoid = jax.nn.sigmoid(gate)
    silu = gate * sigmoid
    act_ref[...] = (silu * up).astype(act_ref.dtype)
    silu_ref[...] = silu.astype(silu_ref.dtype)
    slope_ref[...] = (up * sigmoid * (1.0 + gate * (1.0 - sigmoid))).astype(slope_ref.dtype)


def row_tile(array):
    return pl.BlockSpec((ROWS, array.shape[1]), lambda i, j: (i, 0))


def both_tile():
    return pl.BlockSpec((ROWS, STEP), lambda i, j: (i, j))


def column_tile(array, offset=0):
    return pl.BlockSpec((array.shape[0], STEP), lambda i, j: (0, j + offset))


def hidden_units(x, pair):
    rows, hidden = x.shape[0], pair.shape[1] // 2
    out = jax.ShapeDtypeStruct((rows, hidden), jnp.bfloat16)
    return pl.pallas_call(
        hidden_kernel,
        out_shape=(out, out, out),
        grid=(rows // ROWS, hidden // STEP),
        in_specs=[row_tile(x), column_tile(pair), column_tile(pair, hidden // STEP)],
        out_specs=(both_tile(),) * 3,
        compiler_params=params(),
        cost_estimate=cost(2 * rows * pair.size, [x, pair, out, out, out]),
        name="hidden_units",
    )(x, pair, pair)


def hidden_back_kernel(
    dy_ref, silu_ref, slope_ref, down_ref, gate_ref, up_ref, dgate_ref, dup_ref, dx_ref, total_ref
):
    grad = contract(dy_ref[...], down_ref[...], ((1,), (0,)))
    dup = (grad * silu_ref[...].astype(jnp.float32)).astype(jnp.bfloat16)
    dgate = (grad * slope_ref[...].astype(jnp.float32)).astype(jnp.bfloat16)
    dup_ref[...] = dup
    dgate_ref[...] = dgate
    both = jnp.concatenate([dgate, dup], axis=1)
    weights = jnp.concatenate([gate_ref[...], up_ref[...]], axis=1)
    at, last = pl.program_id(1), pl.num_programs(1) - 1
    term = contract(both, weights, ((1,), (1,)))

    @pl.when(at == 0)
    def _():
        total_ref[...] = term

    @pl.when((at > 0) & (at < last))
    def _():
        total_ref[...] += term

    @pl.when((at > 0) & (at == last))
    def _():
        dx_ref[...] = (total_ref[...] + term).astype(dx_ref.dtype)

    @pl.when((at == 0) & (at == last))
    def _():
        dx_ref[...] = term.astype(dx_ref.dtype)


def hidden_back(dy, silu, slope, down, pair):
    rows, hidden = silu.shape
    out = jax.ShapeDtypeStruct((rows, hidden), jnp.bfloat16)
    out_x = jax.ShapeDtypeStruct(dy.shape, jnp.bfloat16)
    tile = both_tile()
    return pl.pallas_call(
        hidden_back_kernel,
        out_shape=(out, out, out_x),
        grid=(rows // ROWS, hidden // STEP),
        in_specs=[
            row_tile(dy),
            tile,
            tile,
            column_tile(down),
            column_tile(pair),
            column_tile(pair, hidden // STEP),
        ],
        out_specs=(tile, tile, row_tile(dy)),
        scratch_shapes=[pltpu.VMEM((ROWS, dy.shape[1]), jnp.float32)],
        compiler_params=params(),
        cost_estimate=cost(6 * rows * down.size, [dy, silu, slope, down, pair, out, out, dy]),
        name="hidden_back",
    )(dy, silu, slope, down, pair, pair)


def pair_kernel(left_ref, dgate_ref, dup_ref, act_ref, down_ref, term_ref, out_ref):
    hidden = dgate_ref.shape[1]
    left = left_ref[...]
    term_ref[:, :hidden] = contract(left, dgate_ref[...], ((0,), (0,))).astype(term_ref.dtype)
    term_ref[:, hidden:] = contract(left, dup_ref[...], ((0,), (0,))).astype(term_ref.dtype)
    out_ref[...] = contract(act_ref[...], down_ref[...], ((1,), (1,))).astype(out_ref.dtype)


def pair_terms(left, dgate, dup, act, down):
    rows, columns = left.shape
    hidden = act.shape[1]
    term = jax.ShapeDtypeStruct((columns, 2 * hidden), jnp.bfloat16)
    out = jax.ShapeDtypeStruct((rows, columns), jnp.bfloat16)
    return pl.pallas_call(
        pair_kernel,
        out_shape=(term, out),
        grid=(columns // 512,),
        in_specs=[column_block(left, 512)]
        + [whole_block(a) for a in (dgate, dup, act)]
        + [row_block(down, 512)],
        out_specs=(row_block(term, 512), column_block(out, 512)),
        compiler_params=params(),
        cost_estimate=cost(6 * rows * down.size, [left, dgate, dup, act, down, term, out]),
        name="pair_terms",
    )(left, dgate, dup, act, down)


def weight_kernel(left_ref, *refs):
    left, out_ref = left_ref[...], refs[-1]
    start = 0
    for right_ref in refs[:-1]:
        columns = slice(start, start + right_ref.shape[1])
        out_ref[:, columns] = contract(left, right_ref[...], ((0,), (0,))).astype(out_ref.dtype)
        start = columns.stop


def weight_terms(left, *rights):
    rows, columns = left.shape
    out = jax.ShapeDtypeStruct((columns, sum(r.shape[1] for r in rights)), jnp.bfloat16)
    return pl.pallas_call(
        weight_kernel,
        out_shape=out,
        grid=(columns // 512,),
        in_specs=[column_block(left, 512)] + [whole_block(r) for r in rights],
        out_specs=row_block(out, 512),
        compiler_params=params(),
        cost_estimate=cost(2 * rows * out.size, [left, *rights, out]),
        name="weight_terms",
    )(left, *rights)


def attn_weight_kernel(left_ref, right_ref, left2_ref, right2_ref, out_ref):
    columns = right_ref.shape[1]
    first = contract(left_ref[...], right_ref[...], ((0,), (0,)))
    second = contract(left2_ref[...], right2_ref[...], ((0,), (0,)))
    out_ref[:, :columns] = first.astype(out_ref.dtype)
    out_ref[:, columns:] = second.astype(out_ref.dtype)


def attn_weight_terms(left, right, left2, right2):
    columns = left.shape[1]
    out = jax.ShapeDtypeStruct((columns, right.shape[1] + right2.shape[1]), jnp.bfloat16)
    return pl.pallas_call(
        attn_weight_kernel,
        out_shape=out,
        grid=(columns // 512,),
        in_specs=[
            column_block(left, 512),
            whole_block(right),
            column_block(left2, 512),
            whole_block(right2),
        ],
        out_specs=row_block(out, 512),
        compiler_params=params(),
        cost_estimate=cost(2 * left.shape[0] * out.size, [left, right, left2, right2, out]),
        name="attn_weight_terms",
    )(left, right, left2, right2)


def rotate_back(grad_rows, cosine_table, sine_table):
    half_dim = grad_rows.shape[-1] // 2
    scaled = grad_rows * sine_table
    turned = jnp.concatenate([scaled[..., half_dim:], -scaled[..., :half_dim]], axis=-1)
    return grad_rows * cosine_table + turned


def project_back(left, right):
    return jnp.einsum("rf,df->rd", left, right, preferred_element_type=jnp.float32)


def weight_term(left, right):
    return jnp.einsum("rd,rc->dc", left, right, preferred_element_type=jnp.float32)


def after(value, *earlier):
    return lax.optimization_barrier((value, earlier))[0]


def pick(source, index, axis=0):
    return lax.dynamic_index_in_dim(source, index, axis, keepdims=False)


def swap_tensor(value):
    return lax.ppermute(value, "tensor", [(0, 1), (1, 0)])


def shift_ctx(value, distance=1):
    size = lax.axis_size("ctx")
    return lax.ppermute(value, "ctx", [(i, (i + distance) % size) for i in range(size)])


def swap_x(value):
    return lax.ppermute(value, "dp", [(i, i ^ 1) for i in range(4)])


def swap_y(value):
    return lax.ppermute(value, "dp", [(i, i ^ 2) for i in range(4)])


def ring_blocks(value):
    blocks = [value]
    for _ in range(lax.axis_size("ctx") - 1):
        blocks.append(shift_ctx(blocks[-1]))
    return blocks


def direct_blocks(value):
    return [value] + [shift_ctx(value, d) for d in range(1, lax.axis_size("ctx"))]


def direct_terms(blocks):
    sent = [blocks[j].astype(jnp.bfloat16) for j in range(1, len(blocks))]
    return [blocks[0]] + [shift_ctx(block, -j) for j, block in enumerate(sent, 1)]


def sum_terms(terms):
    total = terms[0].astype(jnp.float32)
    for term in terms[1:]:
        total = total + term.astype(jnp.float32)
    return total


def natural_ctx(blocks):
    size = lax.axis_size("ctx")
    own = lax.axis_index("ctx")
    return jnp.stack([lax.select_n((own - c) % size, *blocks) for c in range(size)])


def spread_ctx(columns):
    size = lax.axis_size("ctx")
    own = lax.axis_index("ctx")
    return [pick(columns, own)] + [
        shift_ctx(pick(columns, (own + distance) % size), distance) for distance in range(1, size)
    ]


def in_order(at, own, other):
    return jnp.stack([jnp.where(at == 0, own, other), jnp.where(at == 0, other, own)])


def gather_near_send(value):
    half = value.shape[0] // 2
    first, second = value[:half], value[half:]
    return first, second, swap_x(first), swap_y(second)


def gather_far_send(first, second, got_x, got_y):
    own = lax.axis_index("dp")
    pair_x = in_order(own % 2, first, got_x)
    pair_y = in_order(own // 2, second, got_y)
    return pair_x, pair_y, swap_y(pair_x), swap_x(pair_y)


def gather_whole(pair_x, pair_y, far_x, far_y):
    own = lax.axis_index("dp")
    full_x = in_order(own // 2, pair_x, far_x)
    full_y = jnp.swapaxes(in_order(own % 2, pair_y, far_y), 0, 1)
    return jnp.stack([full_x, full_y], axis=2).reshape(-1, pair_x.shape[-1])


def add(left, right):
    return (left.astype(jnp.float32) + right.astype(jnp.float32)).astype(jnp.bfloat16)


def scatter_near_send(value):
    rows, columns = value.shape[0] // 4, value.shape[1]
    own = lax.axis_index("dp")
    low, high = own % 2, own // 2
    terms = value.reshape(2, 2, 2, rows // 2, columns)
    first, second = terms[:, :, 0], terms[:, :, 1]
    sent_x, sent_y = pick(first, 1 - low, 1), pick(second, 1 - high, 0)
    return pick(first, low, 1), pick(second, high, 0), swap_x(sent_x), swap_y(sent_y)


def scatter_far_send(kept_x, kept_y, got_x, got_y):
    own = lax.axis_index("dp")
    low, high = own % 2, own // 2
    pair_x, pair_y = add(kept_x, got_x), add(kept_y, got_y)
    far_x, far_y = swap_y(pick(pair_x, 1 - high)), swap_x(pick(pair_y, 1 - low))
    return pick(pair_x, high), pick(pair_y, low), far_x, far_y


def scatter_whole(kept_x, kept_y, far_x, far_y):
    whole = jnp.concatenate([add(kept_x, far_x), add(kept_y, far_y)], axis=0)
    return whole.reshape(lax.axis_size("ctx"), -1, whole.shape[1])


def column_parts(weight, ff_part):
    rows, columns = weight.shape
    size = lax.axis_size("ctx")
    wide = jnp.pad(weight.astype(jnp.bfloat16), ((0, 0), (0, size * ff_part - columns)))
    return jnp.stack([wide[:, c * ff_part : (c + 1) * ff_part] for c in range(size)])


def hidden_grad(parts, columns):
    wide = jnp.concatenate([parts[c] for c in range(parts.shape[0])], axis=1)
    return wide[:, :columns].astype(jnp.float32)


def ctx_terms(parts):
    size = lax.axis_size("ctx")
    own = lax.axis_index("ctx")
    return direct_terms([pick(parts, (own - j) % size) for j in range(size)])


def span_rows(blocks):
    mine = jnp.concatenate([b.reshape(-1, b.shape[-1]) for b in blocks], axis=0)
    return jnp.concatenate([mine, swap_tensor(mine)], axis=0)


def core_sum(term):
    half = term.shape[0] // 2
    other = swap_tensor(term[half:].astype(jnp.bfloat16)).astype(jnp.float32)
    mine = (term[:half].astype(jnp.float32) + other).astype(jnp.bfloat16)
    return list(mine.reshape(lax.axis_size("ctx"), -1, mine.shape[1]))


def sum_everywhere(value):
    for axis in ("tensor", "dp", "ctx"):
        size, bit = lax.axis_size(axis), 1
        while bit < size:
            value = value + lax.ppermute(value, axis, [(i, i ^ bit) for i in range(size)])
            bit *= 2
    return value


def per_device(
    tokens,
    prefix,
    w_query,
    w_key,
    w_value,
    w_out,
    w_gate,
    w_up,
    w_down,
    b_query,
    b_key,
    b_value,
    norm_attn,
    norm_mlp,
    cotangent,
):
    bf16, f32 = jnp.bfloat16, jnp.float32
    seq_dev, own_rows, model_width = tokens.shape
    ctx_size = lax.axis_size("ctx")
    span_len = own_rows * 2
    seq_len = span_len * ctx_size
    row_count = seq_dev * span_len
    q_cols = w_query.shape[1]
    kv_cols = w_key.shape[1]
    ff_cols = w_gate.shape[1]
    ff_part = -(-ff_cols // (128 * ctx_size)) * 128
    kv_heads = kv_cols // HD
    group_size = q_cols // kv_cols
    score_scale = HD ** (-0.5)
    tensor_at = lax.axis_index("tensor")
    ctx_at = lax.axis_index("ctx")
    own_pos = jnp.arange(own_rows, dtype=jnp.int32)
    in_span = jnp.concatenate([tensor_at * own_rows + own_pos, (1 - tensor_at) * own_rows + own_pos])
    local_pos = ctx_at * span_len + in_span
    key_pos = jnp.concatenate(
        [((ctx_at - j) % ctx_size) * span_len + in_span for j in range(ctx_size)]
    )
    row_pos, col_pos = local_pos[:, None], key_pos[None, :]
    cosine_table, sine_table = rotary_tables(local_pos)
    cosine_flat, sine_flat = cosine_table[:, 0], sine_table[:, 0]
    bias_query = lax.dynamic_slice_in_dim(b_query, tensor_at * q_cols, q_cols)
    bias_key = lax.dynamic_slice_in_dim(b_key, tensor_at * kv_cols, kv_cols)
    bias_value = lax.dynamic_slice_in_dim(b_value, tensor_at * kv_cols, kv_cols)
    bias_all = jnp.concatenate([bias_query, bias_key, bias_value])
    cast_qkv = jnp.concatenate([w.astype(bf16) for w in (w_query, w_key, w_value)], axis=1)
    qkv_blocks = direct_blocks(cast_qkv)
    out_blocks = direct_blocks(after(w_out, qkv_blocks).astype(bf16))
    x_own = tokens.astype(f32)
    attn_root = inverse_root(x_own)
    normed_own = (x_own * attn_root * norm_attn).astype(bf16)
    normed1 = jnp.concatenate([normed_own, swap_tensor(normed_own)], axis=1).reshape(
        row_count, model_width
    )
    qkv_near = gather_near_send(natural_ctx(qkv_blocks).reshape(-1, cast_qkv.shape[1]))
    pair_parts = jnp.concatenate([column_parts(w, ff_part) for w in (w_gate, w_up)], axis=2)
    pair_blocks = spread_ctx(after(pair_parts, out_blocks))
    qkv_far = gather_far_send(*qkv_near)
    full_qkv = gather_whole(*qkv_far)
    out_near = gather_near_send(after(natural_ctx(out_blocks).reshape(-1, q_cols), qkv_far))
    qkv = qkv_heads(
        normed1,
        full_qkv,
        bias_all[None],
        jnp.tile(cosine_flat, (seq_dev, 1)),
        jnp.tile(sine_flat, (seq_dev, 1)),
        (q_cols + kv_cols) // HD,
    )
    queries = qkv[:, :q_cols]
    out_far = gather_far_send(*after(out_near, qkv))
    pair_blocks = after(pair_blocks, qkv)
    kv_sent = qkv[:, q_cols:].reshape(seq_dev, span_len, 2 * kv_cols)
    kv_blocks = direct_blocks(after(kv_sent, pair_blocks, out_near))
    pair_mine = natural_ctx(pair_blocks).reshape(-1, 2 * ff_part)
    pair_near = gather_near_send(after(pair_mine, out_far))
    kv_rows = jnp.concatenate(after(kv_blocks, pair_mine), axis=1)
    down_blocks = spread_ctx(after(column_parts(w_down, ff_part), kv_blocks))
    mixed_low = attend(prefix, row_pos, col_pos, queries, kv_rows)
    pair_near = after(pair_near, mixed_low)
    pair_far = gather_far_send(*pair_near)
    full_out = gather_whole(*out_far)
    attn_term = project_back(after(mixed_low, pair_near), full_out)
    attn_term = attn_term.reshape(seq_dev, span_len, model_width)
    hidden1 = (
        x_own
        + attn_term[:, :own_rows]
        + swap_tensor(attn_term[:, own_rows:].astype(bf16)).astype(f32)
    )
    mlp_root = inverse_root(hidden1)
    normed2_own = (hidden1 * mlp_root * norm_mlp).astype(bf16)
    down_blocks = after(down_blocks, normed2_own)
    normed2_blocks = direct_blocks(after(normed2_own, down_blocks))
    down_mine = natural_ctx(down_blocks).reshape(-1, ff_part)
    normed2_blocks, pair_far = after((normed2_blocks, pair_far), down_mine)
    cotangent_blocks = direct_blocks(after(cotangent, normed2_blocks))
    down_near = gather_near_send(after(down_mine, pair_far))
    full_pair = gather_whole(*pair_far)
    normed2 = span_rows(normed2_blocks)
    activation, silu, slope = hidden_units(normed2, full_pair)
    down_near, cotangent_blocks = after((down_near, cotangent_blocks), activation)
    down_far = gather_far_send(*down_near)
    grad_mlp = span_rows(cotangent_blocks)
    down_term = weight_terms(grad_mlp, after(activation, down_near))
    down_sums = scatter_near_send(down_term)
    full_down = gather_whole(*after(down_far, down_term))
    down_sums = scatter_far_send(*down_sums)
    grad_gate, grad_up, mlp_back = hidden_back(
        after(grad_mlp, down_sums[:2]), silu, slope, full_down, full_pair
    )
    back_cores = core_sum(mlp_back)
    back_terms = direct_terms(back_cores)
    pair_term, mlp_rows = pair_terms(
        after(normed2, back_cores), grad_gate, grad_up, activation, full_down
    )
    pair_sums = scatter_near_send(pair_term)
    back_terms, down_sums = after((back_terms, down_sums), pair_term)
    down_parts = spread_ctx(after(scatter_whole(*down_sums), back_terms))
    grad_normed2 = sum_terms(back_terms).reshape(tokens.shape)
    grad_out = cotangent.astype(f32)
    scaled2 = norm_mlp * grad_normed2
    grad_hidden1 = (
        grad_out
        + mlp_root * scaled2
        - hidden1 * mlp_root**3 * jnp.mean(scaled2 * hidden1, axis=-1, keepdims=True)
    )
    gain_mlp = jnp.sum(grad_normed2 * hidden1 * mlp_root, axis=(0, 1))
    grad_own = grad_hidden1.astype(bf16)
    grad_attn = jnp.concatenate([grad_own, swap_tensor(grad_own)], axis=1).reshape(
        row_count, model_width
    )
    grad_mixed = jnp.dot(grad_attn, full_out, preferred_element_type=f32).astype(bf16)
    grad_q, kv_terms = attend_back(
        prefix, row_pos, col_pos, queries, kv_rows, grad_mixed, cosine_flat, sine_flat
    )
    down_parts, pair_sums = after((down_parts, pair_sums), kv_terms)
    pair_sums = scatter_far_send(*pair_sums)
    kv_sent = after(kv_terms, down_parts)
    kv_own = direct_terms(
        [kv_sent[:, j * span_len : (j + 1) * span_len] for j in range(ctx_size)]
    )
    mlp_cores = core_sum(after(mlp_rows, back_terms))
    kv_own = after(kv_own, mlp_cores)
    mlp_terms = direct_terms(after(mlp_cores, kv_own))
    kv_sum = sum_terms(kv_own)
    grad_k = rotate_back(kv_sum[:, :, None, :kv_cols], cosine_table, sine_table)
    grad_k = grad_k.reshape(row_count, kv_cols).astype(bf16)
    grad_v = kv_sum[:, :, kv_cols:].reshape(row_count, kv_cols).astype(bf16)
    grad_qkv = jnp.concatenate([grad_q, grad_k, grad_v], axis=1)
    attn_term = attn_weight_terms(normed1, after(grad_qkv, pair_sums), grad_attn, mixed_low)
    attn_sums = scatter_near_send(attn_term)
    grad_w_down = hidden_grad(natural_ctx(down_parts), ff_cols)
    attn_back = project_back(grad_qkv, full_qkv).reshape(seq_dev, span_len, model_width)
    grad_normed1 = attn_back[:, :own_rows] + swap_tensor(
        attn_back[:, own_rows:].astype(bf16)
    ).astype(f32)
    scaled1 = norm_attn * grad_normed1
    grad_tokens = (
        grad_hidden1
        + attn_root * scaled1
        - x_own * attn_root**3 * jnp.mean(scaled1 * x_own, axis=-1, keepdims=True)
    ).astype(bf16)
    attn_sums = scatter_far_send(*after(attn_sums, grad_tokens, mlp_terms))
    output = (hidden1 + sum_terms(mlp_terms).reshape(tokens.shape)).astype(bf16)
    pair_grads = spread_ctx(after(scatter_whole(*pair_sums), mlp_terms))
    gain_attn = jnp.sum(grad_normed1 * x_own * attn_root, axis=(0, 1))
    place_query = lax.dynamic_update_slice_in_dim(
        jnp.zeros_like(b_query), jnp.sum(grad_q, axis=0, dtype=f32), tensor_at * q_cols, 0
    )
    place_key = lax.dynamic_update_slice_in_dim(
        jnp.zeros_like(b_key), jnp.sum(grad_k, axis=0, dtype=f32), tensor_at * kv_cols, 0
    )
    place_value = lax.dynamic_update_slice_in_dim(
        jnp.zeros_like(b_value), jnp.sum(grad_v, axis=0, dtype=f32), tensor_at * kv_cols, 0
    )
    sums = jnp.concatenate([gain_attn, gain_mlp, place_query, place_key, place_value])
    sums = sum_everywhere(after(sums, attn_sums).reshape(-1, 128)).reshape(-1)
    splits = [model_width, 2 * model_width]
    splits += [splits[1] + b_query.shape[0], splits[1] + b_query.shape[0] + b_key.shape[0]]
    sum_attn, sum_mlp, sum_query, sum_key, sum_value = jnp.split(sums, splits)
    attn_grads = sum_terms(ctx_terms(scatter_whole(*attn_sums)))
    grad_w_qkv, grad_w_out = attn_grads[:, :-q_cols], attn_grads[:, -q_cols:]
    pair_grads = natural_ctx(pair_grads)
    grad_w_gate = hidden_grad(pair_grads[:, :, :ff_part], ff_cols)
    grad_w_up = hidden_grad(pair_grads[:, :, ff_part:], ff_cols)
    grad_w_query = grad_w_qkv[:, :q_cols]
    grad_w_key = grad_w_qkv[:, q_cols : q_cols + kv_cols]
    grad_w_value = grad_w_qkv[:, q_cols + kv_cols :]
    return (
        output,
        grad_tokens,
        grad_w_query,
        grad_w_key,
        grad_w_value,
        grad_w_out,
        grad_w_gate,
        grad_w_up,
        grad_w_down,
        sum_query,
        sum_key,
        sum_value,
        sum_attn,
        sum_mlp,
    )


def solution(mesh):
    placed = (
        P("dp", ("ctx", "tensor"), None),
        P("dp"),
        P(("dp", "ctx"), "tensor"),
        P(("dp", "ctx"), "tensor"),
        P(("dp", "ctx"), "tensor"),
        P(("dp", "ctx"), "tensor"),
        P(("dp", "ctx"), "tensor"),
        P(("dp", "ctx"), "tensor"),
        P(("dp", "ctx"), "tensor"),
        P(),
        P(),
        P(),
        P(),
        P(),
        P("dp", ("ctx", "tensor"), None),
    )
    return jax.shard_map(
        per_device,
        mesh=mesh,
        in_specs=placed,
        out_specs=(
            P("dp", ("ctx", "tensor"), None),
            P("dp", ("ctx", "tensor"), None),
            P(("dp", "ctx"), "tensor"),
            P(("dp", "ctx"), "tensor"),
            P(("dp", "ctx"), "tensor"),
            P(("dp", "ctx"), "tensor"),
            P(("dp", "ctx"), "tensor"),
            P(("dp", "ctx"), "tensor"),
            P(("dp", "ctx"), "tensor"),
            P(),
            P(),
            P(),
            P(),
            P(),
        ),
        check_vma=False,
    )
```

```python
import functools

import jax
import jax.numpy as jnp
from jax import lax
from jax.experimental import pallas as pl
from jax.experimental.pallas import tpu as pltpu
from jax.sharding import PartitionSpec as P

HD = 128


epsilon = 1e-06
rope_base = 1000000.0


def inverse_root(value):
    return lax.rsqrt(jnp.mean(value * value, axis=-1, keepdims=True) + epsilon)


def rotary_tables(positions):
    half_dim = HD // 2
    frequency = rope_base ** (-2.0 * jnp.arange(half_dim, dtype=jnp.float32) / HD)
    angles = positions.astype(jnp.float32)[:, None] * frequency[None, :]
    angles = jnp.concatenate([angles, angles], axis=1)
    return (jnp.cos(angles)[:, None, :], jnp.sin(angles)[:, None, :])


VMEM_LIMIT = 44 * 1024 * 1024


def params():
    return pltpu.CompilerParams(vmem_limit_bytes=VMEM_LIMIT)


def cost(flops, arrays):
    moved = sum(a.size * a.dtype.itemsize for a in arrays)
    return pl.CostEstimate(flops=flops, bytes_accessed=moved, transcendentals=0)


def contract(left, right, dims):
    return lax.dot_general(left, right, (dims, ((), ())), preferred_element_type=jnp.float32)


def half_sign(shape):
    return jnp.where(lax.broadcasted_iota(jnp.int32, shape, 1) < shape[1] // 2, 1.0, -1.0)


def qkv_kernel(rope_heads, x_ref, w_ref, b_ref, cos_ref, sin_ref, out_ref):
    at = pl.program_id(0)
    heads = w_ref.shape[1] // HD
    total = contract(x_ref[...], w_ref[...], ((1,), (0,))) + b_ref[...]
    cosine, sine = cos_ref[...], sin_ref[...]
    signed = -half_sign(sine.shape) * sine
    for head in range(heads):
        value = total[:, head * HD : (head + 1) * HD]
        turned = value * cosine + pltpu.roll(value, HD // 2, 1) * signed
        kept = jnp.where(at * heads + head < rope_heads, turned, value)
        out_ref[:, head * HD : (head + 1) * HD] = kept.astype(out_ref.dtype)


def qkv_heads(x, weight, bias, cosine, sine, rope_heads):
    rows, columns = x.shape[0], weight.shape[1]
    out = jax.ShapeDtypeStruct((rows, columns), jnp.bfloat16)
    whole = lambda a: pl.BlockSpec(a.shape, lambda i: (0, 0))
    return pl.pallas_call(
        functools.partial(qkv_kernel, rope_heads),
        out_shape=out,
        grid=(columns // 256,),
        in_specs=[
            whole(x),
            pl.BlockSpec((weight.shape[0], 256), lambda i: (0, i)),
            pl.BlockSpec((1, 256), lambda i: (0, i)),
            whole(cosine),
            whole(sine),
        ],
        out_specs=pl.BlockSpec((rows, 256), lambda i: (0, i)),
        compiler_params=params(),
        cost_estimate=cost(2 * x.size * columns, [x, weight, out]),
        name="qkv_heads",
    )(x, weight, bias, cosine, sine)


def probabilities_of(query, keys, allowed):
    scores = contract(query, keys, ((1,), (1,))) * HD ** (-0.5)
    scores = jnp.where(allowed, scores, -1e30)
    weights = jnp.exp(scores - jnp.max(scores, axis=-1, keepdims=True))
    return weights / jnp.sum(weights, axis=-1, keepdims=True)


def allowed_of(prefix_ref, row_ref, key_ref):
    keys = key_ref[...]
    return (keys <= row_ref[...]) | (keys < prefix_ref[pl.program_id(0)])


def attend_kernel(prefix_ref, row_ref, key_ref, q_ref, kv_ref, out_ref):
    allowed = allowed_of(prefix_ref, row_ref, key_ref)
    keys, values = kv_ref[0, :, :HD], kv_ref[0, :, HD:]
    for head in range(q_ref.shape[1] // HD):
        columns = slice(head * HD, (head + 1) * HD)
        chances = probabilities_of(q_ref[:, columns], keys, allowed).astype(jnp.bfloat16)
        out_ref[:, columns] = contract(chances, values, ((1,), (0,))).astype(out_ref.dtype)


def attend_back_kernel(
    prefix_ref, row_ref, key_ref, q_ref, kv_ref, grad_ref, cos_ref, sin_ref, dq_ref, dkv_ref
):
    allowed = allowed_of(prefix_ref, row_ref, key_ref)
    keys, values = kv_ref[0, :, :HD], kv_ref[0, :, HD:]
    sign = half_sign(cos_ref.shape)
    scale = HD ** (-0.5)
    grad_keys = jnp.zeros(keys.shape, jnp.float32)
    grad_values = jnp.zeros(keys.shape, jnp.float32)
    for head in range(q_ref.shape[1] // HD):
        columns = slice(head * HD, (head + 1) * HD)
        query, grad = q_ref[:, columns], grad_ref[:, columns]
        chances = probabilities_of(query, keys, allowed)
        rounded = chances.astype(jnp.bfloat16)
        grad_chances = contract(grad, values, ((1,), (1,)))
        offset = jnp.sum(rounded.astype(jnp.float32) * grad_chances, axis=-1, keepdims=True)
        grad_scores = (chances * (grad_chances - offset)).astype(jnp.bfloat16)
        turned = contract(grad_scores, keys, ((1,), (0,))) * scale
        back = turned * cos_ref[...] + pltpu.roll(turned * sin_ref[...], HD // 2, 1) * sign
        dq_ref[:, columns] = back.astype(dq_ref.dtype)
        grad_keys += contract(grad_scores, query, ((0,), (0,)))
        grad_values += contract(rounded, grad, ((0,), (0,)))
    dkv_ref[0, :, :HD] = (grad_keys * scale).astype(dkv_ref.dtype)
    dkv_ref[0, :, HD:] = grad_values.astype(dkv_ref.dtype)


def attention_specs(query, kv, row_pos, key_pos):
    rows = query.shape[0] // kv.shape[0]
    heads = pl.BlockSpec((rows, query.shape[1]), lambda i: (i, 0))
    both = pl.BlockSpec((1,) + kv.shape[1:], lambda i: (i, 0, 0))
    return heads, [
        pl.BlockSpec(memory_space=pltpu.SMEM),
        pl.BlockSpec(row_pos.shape, lambda i: (0, 0)),
        pl.BlockSpec(key_pos.shape, lambda i: (0, 0)),
        heads,
        both,
    ], both


def attend(prefix, row_pos, key_pos, query, kv):
    heads, specs, _ = attention_specs(query, kv, row_pos, key_pos)
    return pl.pallas_call(
        attend_kernel,
        out_shape=jax.ShapeDtypeStruct(query.shape, jnp.bfloat16),
        grid=(kv.shape[0],),
        in_specs=specs,
        out_specs=heads,
        compiler_params=params(),
        cost_estimate=cost(4 * query.size * kv.shape[1], [query, kv, query]),
        name="attend",
    )(prefix, row_pos, key_pos, query, kv)


def attend_back(prefix, row_pos, key_pos, query, kv, grad, cosine, sine):
    heads, specs, both = attention_specs(query, kv, row_pos, key_pos)
    table = pl.BlockSpec(cosine.shape, lambda i: (0, 0))
    return pl.pallas_call(
        attend_back_kernel,
        out_shape=(
            jax.ShapeDtypeStruct(query.shape, jnp.bfloat16),
            jax.ShapeDtypeStruct(kv.shape, jnp.bfloat16),
        ),
        grid=(kv.shape[0],),
        in_specs=specs + [heads, table, table],
        out_specs=(heads, both),
        compiler_params=params(),
        cost_estimate=cost(10 * query.size * kv.shape[1], [query, kv, grad, query, kv]),
        name="attend_back",
    )(prefix, row_pos, key_pos, query, kv, grad, cosine, sine)


STEP = 384
ROWS = 1024


def whole_block(array):
    return pl.BlockSpec(array.shape, lambda i: (0, 0))


def column_block(array, columns):
    return pl.BlockSpec((array.shape[0], columns), lambda i: (0, i))


def row_block(array, rows):
    return pl.BlockSpec((rows, array.shape[1]), lambda i: (i, 0))


def hidden_kernel(x_ref, gate_ref, up_ref, act_ref, silu_ref, slope_ref):
    x = x_ref[...]
    gate = contract(x, gate_ref[...], ((1,), (0,)))
    up = contract(x, up_ref[...], ((1,), (0,)))
    sigmoid = jax.nn.sigmoid(gate)
    silu = gate * sigmoid
    act_ref[...] = (silu * up).astype(act_ref.dtype)
    silu_ref[...] = silu.astype(silu_ref.dtype)
    slope_ref[...] = (up * sigmoid * (1.0 + gate * (1.0 - sigmoid))).astype(slope_ref.dtype)


def row_tile(array):
    return pl.BlockSpec((ROWS, array.shape[1]), lambda i, j: (i, 0))


def both_tile():
    return pl.BlockSpec((ROWS, STEP), lambda i, j: (i, j))


def column_tile(array, offset=0):
    return pl.BlockSpec((array.shape[0], STEP), lambda i, j: (0, j + offset))


def hidden_units(x, pair):
    rows, hidden = x.shape[0], pair.shape[1] // 2
    out = jax.ShapeDtypeStruct((rows, hidden), jnp.bfloat16)
    return pl.pallas_call(
        hidden_kernel,
        out_shape=(out, out, out),
        grid=(rows // ROWS, hidden // STEP),
        in_specs=[row_tile(x), column_tile(pair), column_tile(pair, hidden // STEP)],
        out_specs=(both_tile(),) * 3,
        compiler_params=params(),
        cost_estimate=cost(2 * rows * pair.size, [x, pair, out, out, out]),
        name="hidden_units",
    )(x, pair, pair)


def hidden_back_kernel(
    dy_ref, silu_ref, slope_ref, down_ref, gate_ref, up_ref, dgate_ref, dup_ref, dx_ref, total_ref
):
    grad = contract(dy_ref[...], down_ref[...], ((1,), (0,)))
    dup = (grad * silu_ref[...].astype(jnp.float32)).astype(jnp.bfloat16)
    dgate = (grad * slope_ref[...].astype(jnp.float32)).astype(jnp.bfloat16)
    dup_ref[...] = dup
    dgate_ref[...] = dgate
    both = jnp.concatenate([dgate, dup], axis=1)
    weights = jnp.concatenate([gate_ref[...], up_ref[...]], axis=1)
    at, last = pl.program_id(1), pl.num_programs(1) - 1
    term = contract(both, weights, ((1,), (1,)))

    @pl.when(at == 0)
    def _():
        total_ref[...] = term

    @pl.when((at > 0) & (at < last))
    def _():
        total_ref[...] += term

    @pl.when((at > 0) & (at == last))
    def _():
        dx_ref[...] = (total_ref[...] + term).astype(dx_ref.dtype)

    @pl.when((at == 0) & (at == last))
    def _():
        dx_ref[...] = term.astype(dx_ref.dtype)


def hidden_back(dy, silu, slope, down, pair):
    rows, hidden = silu.shape
    out = jax.ShapeDtypeStruct((rows, hidden), jnp.bfloat16)
    out_x = jax.ShapeDtypeStruct(dy.shape, jnp.bfloat16)
    tile = both_tile()
    return pl.pallas_call(
        hidden_back_kernel,
        out_shape=(out, out, out_x),
        grid=(rows // ROWS, hidden // STEP),
        in_specs=[
            row_tile(dy),
            tile,
            tile,
            column_tile(down),
            column_tile(pair),
            column_tile(pair, hidden // STEP),
        ],
        out_specs=(tile, tile, row_tile(dy)),
        scratch_shapes=[pltpu.VMEM((ROWS, dy.shape[1]), jnp.float32)],
        compiler_params=params(),
        cost_estimate=cost(6 * rows * down.size, [dy, silu, slope, down, pair, out, out, dy]),
        name="hidden_back",
    )(dy, silu, slope, down, pair, pair)


def pair_kernel(left_ref, dgate_ref, dup_ref, act_ref, down_ref, term_ref, out_ref):
    hidden = dgate_ref.shape[1]
    left = left_ref[...]
    term_ref[:, :hidden] = contract(left, dgate_ref[...], ((0,), (0,))).astype(term_ref.dtype)
    term_ref[:, hidden:] = contract(left, dup_ref[...], ((0,), (0,))).astype(term_ref.dtype)
    out_ref[...] = contract(act_ref[...], down_ref[...], ((1,), (1,))).astype(out_ref.dtype)


def pair_terms(left, dgate, dup, act, down):
    rows, columns = left.shape
    hidden = act.shape[1]
    term = jax.ShapeDtypeStruct((columns, 2 * hidden), jnp.bfloat16)
    out = jax.ShapeDtypeStruct((rows, columns), jnp.bfloat16)
    return pl.pallas_call(
        pair_kernel,
        out_shape=(term, out),
        grid=(columns // 512,),
        in_specs=[column_block(left, 512)]
        + [whole_block(a) for a in (dgate, dup, act)]
        + [row_block(down, 512)],
        out_specs=(row_block(term, 512), column_block(out, 512)),
        compiler_params=params(),
        cost_estimate=cost(6 * rows * down.size, [left, dgate, dup, act, down, term, out]),
        name="pair_terms",
    )(left, dgate, dup, act, down)


def weight_kernel(left_ref, *refs):
    left, out_ref = left_ref[...], refs[-1]
    start = 0
    for right_ref in refs[:-1]:
        columns = slice(start, start + right_ref.shape[1])
        out_ref[:, columns] = contract(left, right_ref[...], ((0,), (0,))).astype(out_ref.dtype)
        start = columns.stop


def weight_terms(left, *rights):
    rows, columns = left.shape
    out = jax.ShapeDtypeStruct((columns, sum(r.shape[1] for r in rights)), jnp.bfloat16)
    return pl.pallas_call(
        weight_kernel,
        out_shape=out,
        grid=(columns // 512,),
        in_specs=[column_block(left, 512)] + [whole_block(r) for r in rights],
        out_specs=row_block(out, 512),
        compiler_params=params(),
        cost_estimate=cost(2 * rows * out.size, [left, *rights, out]),
        name="weight_terms",
    )(left, *rights)


def attn_weight_kernel(left_ref, right_ref, left2_ref, right2_ref, out_ref):
    columns = right_ref.shape[1]
    first = contract(left_ref[...], right_ref[...], ((0,), (0,)))
    second = contract(left2_ref[...], right2_ref[...], ((0,), (0,)))
    out_ref[:, :columns] = first.astype(out_ref.dtype)
    out_ref[:, columns:] = second.astype(out_ref.dtype)


def attn_weight_terms(left, right, left2, right2):
    columns = left.shape[1]
    out = jax.ShapeDtypeStruct((columns, right.shape[1] + right2.shape[1]), jnp.bfloat16)
    return pl.pallas_call(
        attn_weight_kernel,
        out_shape=out,
        grid=(columns // 512,),
        in_specs=[
            column_block(left, 512),
            whole_block(right),
            column_block(left2, 512),
            whole_block(right2),
        ],
        out_specs=row_block(out, 512),
        compiler_params=params(),
        cost_estimate=cost(2 * left.shape[0] * out.size, [left, right, left2, right2, out]),
        name="attn_weight_terms",
    )(left, right, left2, right2)


def rotate_back(grad_rows, cosine_table, sine_table):
    half_dim = grad_rows.shape[-1] // 2
    scaled = grad_rows * sine_table
    turned = jnp.concatenate([scaled[..., half_dim:], -scaled[..., :half_dim]], axis=-1)
    return grad_rows * cosine_table + turned


def project_back(left, right):
    return jnp.einsum("rf,df->rd", left, right, preferred_element_type=jnp.float32)


def weight_term(left, right):
    return jnp.einsum("rd,rc->dc", left, right, preferred_element_type=jnp.float32)


def after(value, *earlier):
    return lax.optimization_barrier((value, earlier))[0]


def pick(source, index, axis=0):
    return lax.dynamic_index_in_dim(source, index, axis, keepdims=False)


def swap_tensor(value):
    return lax.ppermute(value, "tensor", [(0, 1), (1, 0)])


def shift_ctx(value, distance=1):
    size = lax.axis_size("ctx")
    return lax.ppermute(value, "ctx", [(i, (i + distance) % size) for i in range(size)])


def swap_x(value):
    return lax.ppermute(value, "dp", [(i, i ^ 1) for i in range(4)])


def swap_y(value):
    return lax.ppermute(value, "dp", [(i, i ^ 2) for i in range(4)])


def ring_blocks(value):
    blocks = [value]
    for _ in range(lax.axis_size("ctx") - 1):
        blocks.append(shift_ctx(blocks[-1]))
    return blocks


def direct_blocks(value):
    return [value] + [shift_ctx(value, d) for d in range(1, lax.axis_size("ctx"))]


def direct_terms(blocks):
    sent = [blocks[j].astype(jnp.bfloat16) for j in range(1, len(blocks))]
    return [blocks[0]] + [shift_ctx(block, -j) for j, block in enumerate(sent, 1)]


def sum_terms(terms):
    total = terms[0].astype(jnp.float32)
    for term in terms[1:]:
        total = total + term.astype(jnp.float32)
    return total


def natural_ctx(blocks):
    size = lax.axis_size("ctx")
    own = lax.axis_index("ctx")
    return jnp.stack([lax.select_n((own - c) % size, *blocks) for c in range(size)])


def spread_ctx(columns):
    size = lax.axis_size("ctx")
    own = lax.axis_index("ctx")
    return [pick(columns, own)] + [
        shift_ctx(pick(columns, (own + distance) % size), distance) for distance in range(1, size)
    ]


def in_order(at, own, other):
    return jnp.stack([jnp.where(at == 0, own, other), jnp.where(at == 0, other, own)])


def gather_near_send(value):
    half = value.shape[0] // 2
    first, second = value[:half], value[half:]
    return first, second, swap_x(first), swap_y(second)


def gather_far_send(first, second, got_x, got_y):
    own = lax.axis_index("dp")
    pair_x = in_order(own % 2, first, got_x)
    pair_y = in_order(own // 2, second, got_y)
    return pair_x, pair_y, swap_y(pair_x), swap_x(pair_y)


def gather_whole(pair_x, pair_y, far_x, far_y):
    own = lax.axis_index("dp")
    full_x = in_order(own // 2, pair_x, far_x)
    full_y = jnp.swapaxes(in_order(own % 2, pair_y, far_y), 0, 1)
    return jnp.stack([full_x, full_y], axis=2).reshape(-1, pair_x.shape[-1])


def add(left, right):
    return (left.astype(jnp.float32) + right.astype(jnp.float32)).astype(jnp.bfloat16)


def scatter_near_send(value):
    rows, columns = value.shape[0] // 4, value.shape[1]
    own = lax.axis_index("dp")
    low, high = own % 2, own // 2
    terms = value.reshape(2, 2, 2, rows // 2, columns)
    first, second = terms[:, :, 0], terms[:, :, 1]
    sent_x, sent_y = pick(first, 1 - low, 1), pick(second, 1 - high, 0)
    return pick(first, low, 1), pick(second, high, 0), swap_x(sent_x), swap_y(sent_y)


def scatter_far_send(kept_x, kept_y, got_x, got_y):
    own = lax.axis_index("dp")
    low, high = own % 2, own // 2
    pair_x, pair_y = add(kept_x, got_x), add(kept_y, got_y)
    far_x, far_y = swap_y(pick(pair_x, 1 - high)), swap_x(pick(pair_y, 1 - low))
    return pick(pair_x, high), pick(pair_y, low), far_x, far_y


def scatter_whole(kept_x, kept_y, far_x, far_y):
    whole = jnp.concatenate([add(kept_x, far_x), add(kept_y, far_y)], axis=0)
    return whole.reshape(lax.axis_size("ctx"), -1, whole.shape[1])


def column_parts(weight, ff_part):
    rows, columns = weight.shape
    size = lax.axis_size("ctx")
    wide = jnp.pad(weight.astype(jnp.bfloat16), ((0, 0), (0, size * ff_part - columns)))
    return jnp.stack([wide[:, c * ff_part : (c + 1) * ff_part] for c in range(size)])


def hidden_grad(parts, columns):
    wide = jnp.concatenate([parts[c] for c in range(parts.shape[0])], axis=1)
    return wide[:, :columns].astype(jnp.float32)


def ctx_terms(parts):
    size = lax.axis_size("ctx")
    own = lax.axis_index("ctx")
    return direct_terms([pick(parts, (own - j) % size) for j in range(size)])


def span_rows(blocks):
    mine = jnp.concatenate([b.reshape(-1, b.shape[-1]) for b in blocks], axis=0)
    return jnp.concatenate([mine, swap_tensor(mine)], axis=0)


def core_sum(term):
    half = term.shape[0] // 2
    other = swap_tensor(term[half:].astype(jnp.bfloat16)).astype(jnp.float32)
    mine = (term[:half].astype(jnp.float32) + other).astype(jnp.bfloat16)
    return list(mine.reshape(lax.axis_size("ctx"), -1, mine.shape[1]))


def sum_everywhere(value):
    for axis in ("dp", "ctx"):
        size, bit = lax.axis_size(axis), 1
        while bit < size:
            value = value + lax.ppermute(value, axis, [(i, i ^ bit) for i in range(size)])
            bit *= 2
    return value


def per_device(
    tokens,
    prefix,
    w_query,
    w_key,
    w_value,
    w_out,
    w_gate,
    w_up,
    w_down,
    b_query,
    b_key,
    b_value,
    norm_attn,
    norm_mlp,
    cotangent,
):
    bf16, f32 = jnp.bfloat16, jnp.float32
    seq_dev, own_rows, model_width = tokens.shape
    ctx_size = lax.axis_size("ctx")
    span_len = own_rows * 2
    seq_len = span_len * ctx_size
    row_count = seq_dev * span_len
    q_cols = w_query.shape[1]
    kv_cols = w_key.shape[1]
    ff_cols = w_gate.shape[1]
    ff_part = -(-ff_cols // (128 * ctx_size)) * 128
    kv_heads = kv_cols // HD
    group_size = q_cols // kv_cols
    score_scale = HD ** (-0.5)
    tensor_at = lax.axis_index("tensor")
    ctx_at = lax.axis_index("ctx")
    own_pos = jnp.arange(own_rows, dtype=jnp.int32)
    in_span = jnp.concatenate([tensor_at * own_rows + own_pos, (1 - tensor_at) * own_rows + own_pos])
    local_pos = ctx_at * span_len + in_span
    key_pos = jnp.concatenate(
        [((ctx_at - j) % ctx_size) * span_len + in_span for j in range(ctx_size)]
    )
    row_pos, col_pos = local_pos[:, None], key_pos[None, :]
    cosine_table, sine_table = rotary_tables(local_pos)
    cosine_flat, sine_flat = cosine_table[:, 0], sine_table[:, 0]
    bias_query = lax.dynamic_slice_in_dim(b_query, tensor_at * q_cols, q_cols)
    bias_key = lax.dynamic_slice_in_dim(b_key, tensor_at * kv_cols, kv_cols)
    bias_value = lax.dynamic_slice_in_dim(b_value, tensor_at * kv_cols, kv_cols)
    bias_all = jnp.concatenate([bias_query, bias_key, bias_value])
    cast_qkv = jnp.concatenate([w.astype(bf16) for w in (w_query, w_key, w_value)], axis=1)
    qkv_blocks = direct_blocks(cast_qkv)
    out_blocks = direct_blocks(after(w_out, qkv_blocks).astype(bf16))
    x_own = tokens.astype(f32)
    attn_root = inverse_root(x_own)
    normed_own = (x_own * attn_root * norm_attn).astype(bf16)
    normed1 = jnp.concatenate([normed_own, swap_tensor(normed_own)], axis=1).reshape(
        row_count, model_width
    )
    qkv_near = gather_near_send(natural_ctx(qkv_blocks).reshape(-1, cast_qkv.shape[1]))
    pair_parts = jnp.concatenate([column_parts(w, ff_part) for w in (w_gate, w_up)], axis=2)
    pair_blocks = spread_ctx(after(pair_parts, out_blocks))
    qkv_far = gather_far_send(*qkv_near)
    full_qkv = gather_whole(*qkv_far)
    out_near = gather_near_send(after(natural_ctx(out_blocks).reshape(-1, q_cols), qkv_far))
    qkv = qkv_heads(
        normed1,
        full_qkv,
        bias_all[None],
        jnp.tile(cosine_flat, (seq_dev, 1)),
        jnp.tile(sine_flat, (seq_dev, 1)),
        (q_cols + kv_cols) // HD,
    )
    queries = qkv[:, :q_cols]
    out_far = gather_far_send(*after(out_near, qkv))
    pair_blocks = after(pair_blocks, qkv)
    kv_sent = qkv[:, q_cols:].reshape(seq_dev, span_len, 2 * kv_cols)
    kv_blocks = direct_blocks(after(kv_sent, pair_blocks, out_near))
    pair_mine = natural_ctx(pair_blocks).reshape(-1, 2 * ff_part)
    kv_blocks = after(kv_blocks, pair_mine)
    out_far = after(out_far, kv_blocks)
    pair_near = gather_near_send(after(pair_mine, out_far))
    kv_rows = jnp.concatenate(kv_blocks, axis=1)
    mixed_low = attend(prefix, row_pos, col_pos, queries, kv_rows)
    full_out = gather_whole(*out_far)
    attn_term = project_back(mixed_low, full_out)
    attn_term = attn_term.reshape(seq_dev, span_len, model_width)
    hidden1 = (
        x_own
        + attn_term[:, :own_rows]
        + swap_tensor(attn_term[:, own_rows:].astype(bf16)).astype(f32)
    )
    mlp_root = inverse_root(hidden1)
    normed2_own = (hidden1 * mlp_root * norm_mlp).astype(bf16)
    normed2_blocks = direct_blocks(normed2_own)
    pair_far = gather_far_send(*after(pair_near, normed2_own))
    normed2 = span_rows(after(normed2_blocks, pair_far[:2]))
    down_blocks = spread_ctx(after(column_parts(w_down, ff_part), normed2))
    down_mine = natural_ctx(down_blocks).reshape(-1, ff_part)
    cotangent_blocks = direct_blocks(after(cotangent, down_blocks))
    pair_far = after(pair_far, down_mine)
    down_near = gather_near_send(after(down_mine, pair_far))
    full_pair = gather_whole(*pair_far)
    activation, silu, slope = hidden_units(normed2, full_pair)
    down_near, cotangent_blocks = after((down_near, cotangent_blocks), activation)
    down_far = gather_far_send(*down_near)
    grad_mlp = span_rows(cotangent_blocks)
    down_term = weight_terms(grad_mlp, after(activation, down_near))
    down_sums = scatter_near_send(down_term)
    full_down = gather_whole(*after(down_far, down_term))
    grad_gate, grad_up, mlp_back = hidden_back(
        after(grad_mlp, down_term), silu, slope, full_down, full_pair
    )
    back_cores = core_sum(mlp_back)
    back_terms = direct_terms(back_cores)
    pair_term, mlp_rows = pair_terms(
        after(normed2, back_cores), grad_gate, grad_up, activation, full_down
    )
    pair_sums = scatter_near_send(pair_term)
    down_sums = scatter_far_send(*after(down_sums, pair_term))
    back_terms = after(back_terms, pair_term)
    mlp_cores = core_sum(after(mlp_rows, pair_term))
    back_terms, down_sums = after((back_terms, down_sums), mlp_cores)
    down_parts = spread_ctx(after(scatter_whole(*down_sums), back_terms))
    grad_normed2 = sum_terms(back_terms).reshape(tokens.shape)
    grad_out = cotangent.astype(f32)
    scaled2 = norm_mlp * grad_normed2
    grad_hidden1 = (
        grad_out
        + mlp_root * scaled2
        - hidden1 * mlp_root**3 * jnp.mean(scaled2 * hidden1, axis=-1, keepdims=True)
    )
    gain_mlp = jnp.sum(grad_normed2 * hidden1 * mlp_root, axis=(0, 1))
    grad_own = grad_hidden1.astype(bf16)
    grad_attn = jnp.concatenate([grad_own, swap_tensor(grad_own)], axis=1).reshape(
        row_count, model_width
    )
    grad_mixed = jnp.dot(grad_attn, full_out, preferred_element_type=f32).astype(bf16)
    grad_q, kv_terms = attend_back(
        prefix, row_pos, col_pos, queries, kv_rows, grad_mixed, cosine_flat, sine_flat
    )
    down_parts = after(down_parts, kv_terms)
    kv_sent = after(kv_terms, down_parts)
    pair_sums = scatter_far_send(*after(pair_sums, kv_sent))
    kv_own = direct_terms(
        [kv_sent[:, j * span_len : (j + 1) * span_len] for j in range(ctx_size)]
    )
    mlp_terms = direct_terms(after(mlp_cores, kv_own))
    kv_sum = sum_terms(kv_own)
    grad_k = rotate_back(kv_sum[:, :, None, :kv_cols], cosine_table, sine_table)
    grad_k = grad_k.reshape(row_count, kv_cols).astype(bf16)
    grad_v = kv_sum[:, :, kv_cols:].reshape(row_count, kv_cols).astype(bf16)
    grad_qkv = jnp.concatenate([grad_q, grad_k, grad_v], axis=1)
    attn_term = attn_weight_terms(normed1, after(grad_qkv, pair_sums), grad_attn, mixed_low)
    attn_sums = scatter_near_send(attn_term)
    mlp_terms = after(mlp_terms, attn_term)
    grad_w_down = hidden_grad(natural_ctx(down_parts), ff_cols)
    attn_back = project_back(grad_qkv, full_qkv).reshape(seq_dev, span_len, model_width)
    grad_normed1 = attn_back[:, :own_rows] + swap_tensor(
        attn_back[:, own_rows:].astype(bf16)
    ).astype(f32)
    scaled1 = norm_attn * grad_normed1
    grad_tokens = (
        grad_hidden1
        + attn_root * scaled1
        - x_own * attn_root**3 * jnp.mean(scaled1 * x_own, axis=-1, keepdims=True)
    ).astype(bf16)
    attn_sums = scatter_far_send(*after(attn_sums, grad_tokens))
    output = (hidden1 + sum_terms(mlp_terms).reshape(tokens.shape)).astype(bf16)
    pair_grads = spread_ctx(after(scatter_whole(*pair_sums), mlp_terms, attn_sums[:2]))
    gain_attn = jnp.sum(grad_normed1 * x_own * attn_root, axis=(0, 1))
    place_query = lax.dynamic_update_slice_in_dim(
        jnp.zeros_like(b_query), jnp.sum(grad_q, axis=0, dtype=f32), tensor_at * q_cols, 0
    )
    place_key = lax.dynamic_update_slice_in_dim(
        jnp.zeros_like(b_key), jnp.sum(grad_k, axis=0, dtype=f32), tensor_at * kv_cols, 0
    )
    place_value = lax.dynamic_update_slice_in_dim(
        jnp.zeros_like(b_value), jnp.sum(grad_v, axis=0, dtype=f32), tensor_at * kv_cols, 0
    )
    sums = jnp.concatenate([gain_attn, gain_mlp, place_query, place_key, place_value])
    attn_terms = ctx_terms(scatter_whole(*after(attn_sums, pair_grads[1])))
    sums = after(sums, attn_terms[1]).reshape(-1, 128)
    sums = sum_everywhere(sums + swap_tensor(sums)).reshape(-1)
    splits = [model_width, 2 * model_width]
    splits += [splits[1] + b_query.shape[0], splits[1] + b_query.shape[0] + b_key.shape[0]]
    sum_attn, sum_mlp, sum_query, sum_key, sum_value = jnp.split(sums, splits)
    attn_grads = sum_terms(attn_terms)
    grad_w_qkv, grad_w_out = attn_grads[:, :-q_cols], attn_grads[:, -q_cols:]
    pair_grads = natural_ctx(pair_grads)
    grad_w_gate = hidden_grad(pair_grads[:, :, :ff_part], ff_cols)
    grad_w_up = hidden_grad(pair_grads[:, :, ff_part:], ff_cols)
    grad_w_query = grad_w_qkv[:, :q_cols]
    grad_w_key = grad_w_qkv[:, q_cols : q_cols + kv_cols]
    grad_w_value = grad_w_qkv[:, q_cols + kv_cols :]
    return (
        output,
        grad_tokens,
        grad_w_query,
        grad_w_key,
        grad_w_value,
        grad_w_out,
        grad_w_gate,
        grad_w_up,
        grad_w_down,
        sum_query,
        sum_key,
        sum_value,
        sum_attn,
        sum_mlp,
    )


def solution(mesh):
    placed = (
        P("dp", ("ctx", "tensor"), None),
        P("dp"),
        P(("dp", "ctx"), "tensor"),
        P(("dp", "ctx"), "tensor"),
        P(("dp", "ctx"), "tensor"),
        P(("dp", "ctx"), "tensor"),
        P(("dp", "ctx"), "tensor"),
        P(("dp", "ctx"), "tensor"),
        P(("dp", "ctx"), "tensor"),
        P(),
        P(),
        P(),
        P(),
        P(),
        P("dp", ("ctx", "tensor"), None),
    )
    return jax.shard_map(
        per_device,
        mesh=mesh,
        in_specs=placed,
        out_specs=(
            P("dp", ("ctx", "tensor"), None),
            P("dp", ("ctx", "tensor"), None),
            P(("dp", "ctx"), "tensor"),
            P(("dp", "ctx"), "tensor"),
            P(("dp", "ctx"), "tensor"),
            P(("dp", "ctx"), "tensor"),
            P(("dp", "ctx"), "tensor"),
            P(("dp", "ctx"), "tensor"),
            P(("dp", "ctx"), "tensor"),
            P(),
            P(),
            P(),
            P(),
            P(),
        ),
        check_vma=False,
    )
```

```python
import functools

import jax
import jax.numpy as jnp
from jax import lax
from jax.experimental import pallas as pl
from jax.experimental.pallas import tpu as pltpu
from jax.sharding import PartitionSpec as P

HD = 128


epsilon = 1e-06
rope_base = 1000000.0


def inverse_root(value):
    return lax.rsqrt(jnp.mean(value * value, axis=-1, keepdims=True) + epsilon)


def rotary_tables(positions):
    half_dim = HD // 2
    frequency = rope_base ** (-2.0 * jnp.arange(half_dim, dtype=jnp.float32) / HD)
    angles = positions.astype(jnp.float32)[:, None] * frequency[None, :]
    angles = jnp.concatenate([angles, angles], axis=1)
    return (jnp.cos(angles)[:, None, :], jnp.sin(angles)[:, None, :])


VMEM_LIMIT = 32 * 1024 * 1024


def params():
    return pltpu.CompilerParams(vmem_limit_bytes=VMEM_LIMIT)


def cost(flops, arrays):
    moved = sum(a.size * a.dtype.itemsize for a in arrays)
    return pl.CostEstimate(flops=flops, bytes_accessed=moved, transcendentals=0)


def contract(left, right, dims):
    return lax.dot_general(left, right, (dims, ((), ())), preferred_element_type=jnp.float32)


def half_sign(shape):
    return jnp.where(lax.broadcasted_iota(jnp.int32, shape, 1) < shape[1] // 2, 1.0, -1.0)


def qkv_kernel(rope_heads, x_ref, w_ref, b_ref, cos_ref, sin_ref, out_ref):
    at = pl.program_id(0)
    heads = w_ref.shape[1] // HD
    total = contract(x_ref[...], w_ref[...], ((1,), (0,))) + b_ref[...]
    cosine, sine = cos_ref[...], sin_ref[...]
    signed = -half_sign(sine.shape) * sine
    for head in range(heads):
        value = total[:, head * HD : (head + 1) * HD]
        turned = value * cosine + pltpu.roll(value, HD // 2, 1) * signed
        kept = jnp.where(at * heads + head < rope_heads, turned, value)
        out_ref[:, head * HD : (head + 1) * HD] = kept.astype(out_ref.dtype)


def qkv_heads(x, weight, bias, cosine, sine, rope_heads):
    rows, columns = x.shape[0], weight.shape[1]
    out = jax.ShapeDtypeStruct((rows, columns), jnp.bfloat16)
    whole = lambda a: pl.BlockSpec(a.shape, lambda i: (0, 0))
    return pl.pallas_call(
        functools.partial(qkv_kernel, rope_heads),
        out_shape=out,
        grid=(columns // 256,),
        in_specs=[
            whole(x),
            pl.BlockSpec((weight.shape[0], 256), lambda i: (0, i)),
            pl.BlockSpec((1, 256), lambda i: (0, i)),
            whole(cosine),
            whole(sine),
        ],
        out_specs=pl.BlockSpec((rows, 256), lambda i: (0, i)),
        compiler_params=params(),
        cost_estimate=cost(2 * x.size * columns, [x, weight, out]),
        name="qkv_heads",
    )(x, weight, bias, cosine, sine)


def probabilities_of(query, keys, allowed):
    scores = contract(query, keys, ((1,), (1,))) * HD ** (-0.5)
    scores = jnp.where(allowed, scores, -1e30)
    weights = jnp.exp(scores - jnp.max(scores, axis=-1, keepdims=True))
    return weights / jnp.sum(weights, axis=-1, keepdims=True)


def allowed_of(prefix_ref, row_ref, key_ref):
    keys = key_ref[...]
    return (keys <= row_ref[...]) | (keys < prefix_ref[pl.program_id(0)])


def attend_kernel(prefix_ref, row_ref, key_ref, q_ref, kv_ref, out_ref):
    allowed = allowed_of(prefix_ref, row_ref, key_ref)
    keys, values = kv_ref[0, :, :HD], kv_ref[0, :, HD:]
    for head in range(q_ref.shape[1] // HD):
        columns = slice(head * HD, (head + 1) * HD)
        chances = probabilities_of(q_ref[:, columns], keys, allowed).astype(jnp.bfloat16)
        out_ref[:, columns] = contract(chances, values, ((1,), (0,))).astype(out_ref.dtype)


def attend_back_kernel(
    prefix_ref, row_ref, key_ref, q_ref, kv_ref, grad_ref, cos_ref, sin_ref, dq_ref, dkv_ref
):
    allowed = allowed_of(prefix_ref, row_ref, key_ref)
    keys, values = kv_ref[0, :, :HD], kv_ref[0, :, HD:]
    sign = half_sign(cos_ref.shape)
    scale = HD ** (-0.5)
    grad_keys = jnp.zeros(keys.shape, jnp.float32)
    grad_values = jnp.zeros(keys.shape, jnp.float32)
    for head in range(q_ref.shape[1] // HD):
        columns = slice(head * HD, (head + 1) * HD)
        query, grad = q_ref[:, columns], grad_ref[:, columns]
        chances = probabilities_of(query, keys, allowed)
        rounded = chances.astype(jnp.bfloat16)
        grad_chances = contract(grad, values, ((1,), (1,)))
        offset = jnp.sum(rounded.astype(jnp.float32) * grad_chances, axis=-1, keepdims=True)
        grad_scores = (chances * (grad_chances - offset)).astype(jnp.bfloat16)
        turned = contract(grad_scores, keys, ((1,), (0,))) * scale
        back = turned * cos_ref[...] + pltpu.roll(turned * sin_ref[...], HD // 2, 1) * sign
        dq_ref[:, columns] = back.astype(dq_ref.dtype)
        grad_keys += contract(grad_scores, query, ((0,), (0,)))
        grad_values += contract(rounded, grad, ((0,), (0,)))
    dkv_ref[0, :, :HD] = (grad_keys * scale).astype(dkv_ref.dtype)
    dkv_ref[0, :, HD:] = grad_values.astype(dkv_ref.dtype)


def attention_specs(query, kv, row_pos, key_pos):
    rows = query.shape[0] // kv.shape[0]
    heads = pl.BlockSpec((rows, query.shape[1]), lambda i: (i, 0))
    both = pl.BlockSpec((1,) + kv.shape[1:], lambda i: (i, 0, 0))
    return heads, [
        pl.BlockSpec(memory_space=pltpu.SMEM),
        pl.BlockSpec(row_pos.shape, lambda i: (0, 0)),
        pl.BlockSpec(key_pos.shape, lambda i: (0, 0)),
        heads,
        both,
    ], both


def attend(prefix, row_pos, key_pos, query, kv):
    heads, specs, _ = attention_specs(query, kv, row_pos, key_pos)
    return pl.pallas_call(
        attend_kernel,
        out_shape=jax.ShapeDtypeStruct(query.shape, jnp.bfloat16),
        grid=(kv.shape[0],),
        in_specs=specs,
        out_specs=heads,
        compiler_params=params(),
        cost_estimate=cost(4 * query.size * kv.shape[1], [query, kv, query]),
        name="attend",
    )(prefix, row_pos, key_pos, query, kv)


def attend_back(prefix, row_pos, key_pos, query, kv, grad, cosine, sine):
    heads, specs, both = attention_specs(query, kv, row_pos, key_pos)
    table = pl.BlockSpec(cosine.shape, lambda i: (0, 0))
    return pl.pallas_call(
        attend_back_kernel,
        out_shape=(
            jax.ShapeDtypeStruct(query.shape, jnp.bfloat16),
            jax.ShapeDtypeStruct(kv.shape, jnp.bfloat16),
        ),
        grid=(kv.shape[0],),
        in_specs=specs + [heads, table, table],
        out_specs=(heads, both),
        compiler_params=params(),
        cost_estimate=cost(10 * query.size * kv.shape[1], [query, kv, grad, query, kv]),
        name="attend_back",
    )(prefix, row_pos, key_pos, query, kv, grad, cosine, sine)


STEP = 384
ROWS = 1024


def whole_block(array):
    return pl.BlockSpec(array.shape, lambda i: (0, 0))


def column_block(array, columns):
    return pl.BlockSpec((array.shape[0], columns), lambda i: (0, i))


def row_block(array, rows):
    return pl.BlockSpec((rows, array.shape[1]), lambda i: (i, 0))


def hidden_kernel(x_ref, gate_ref, up_ref, act_ref, silu_ref, slope_ref):
    x = x_ref[...]
    gate = contract(x, gate_ref[...], ((1,), (0,)))
    up = contract(x, up_ref[...], ((1,), (0,)))
    sigmoid = jax.nn.sigmoid(gate)
    silu = gate * sigmoid
    act_ref[...] = (silu * up).astype(act_ref.dtype)
    silu_ref[...] = silu.astype(silu_ref.dtype)
    slope_ref[...] = (up * sigmoid * (1.0 + gate * (1.0 - sigmoid))).astype(slope_ref.dtype)


def row_tile(array):
    return pl.BlockSpec((ROWS, array.shape[1]), lambda i, j: (i, 0))


def both_tile():
    return pl.BlockSpec((ROWS, STEP), lambda i, j: (i, j))


def column_tile(array, offset=0):
    return pl.BlockSpec((array.shape[0], STEP), lambda i, j: (0, j + offset))


def hidden_units(x, pair):
    rows, hidden = x.shape[0], pair.shape[1] // 2
    out = jax.ShapeDtypeStruct((rows, hidden), jnp.bfloat16)
    return pl.pallas_call(
        hidden_kernel,
        out_shape=(out, out, out),
        grid=(rows // ROWS, hidden // STEP),
        in_specs=[row_tile(x), column_tile(pair), column_tile(pair, hidden // STEP)],
        out_specs=(both_tile(),) * 3,
        compiler_params=params(),
        cost_estimate=cost(2 * rows * pair.size, [x, pair, out, out, out]),
        name="hidden_units",
    )(x, pair, pair)


def hidden_back_kernel(
    dy_ref, silu_ref, slope_ref, down_ref, gate_ref, up_ref, dgate_ref, dup_ref, dx_ref, total_ref
):
    grad = contract(dy_ref[...], down_ref[...], ((1,), (0,)))
    dup = (grad * silu_ref[...].astype(jnp.float32)).astype(jnp.bfloat16)
    dgate = (grad * slope_ref[...].astype(jnp.float32)).astype(jnp.bfloat16)
    dup_ref[...] = dup
    dgate_ref[...] = dgate
    both = jnp.concatenate([dgate, dup], axis=1)
    weights = jnp.concatenate([gate_ref[...], up_ref[...]], axis=1)
    at, last = pl.program_id(1), pl.num_programs(1) - 1
    term = contract(both, weights, ((1,), (1,)))

    @pl.when(at == 0)
    def _():
        total_ref[...] = term

    @pl.when((at > 0) & (at < last))
    def _():
        total_ref[...] += term

    @pl.when((at > 0) & (at == last))
    def _():
        dx_ref[...] = (total_ref[...] + term).astype(dx_ref.dtype)

    @pl.when((at == 0) & (at == last))
    def _():
        dx_ref[...] = term.astype(dx_ref.dtype)


def hidden_back(dy, silu, slope, down, pair):
    rows, hidden = silu.shape
    out = jax.ShapeDtypeStruct((rows, hidden), jnp.bfloat16)
    out_x = jax.ShapeDtypeStruct(dy.shape, jnp.bfloat16)
    tile = both_tile()
    return pl.pallas_call(
        hidden_back_kernel,
        out_shape=(out, out, out_x),
        grid=(rows // ROWS, hidden // STEP),
        in_specs=[
            row_tile(dy),
            tile,
            tile,
            column_tile(down),
            column_tile(pair),
            column_tile(pair, hidden // STEP),
        ],
        out_specs=(tile, tile, row_tile(dy)),
        scratch_shapes=[pltpu.VMEM((ROWS, dy.shape[1]), jnp.float32)],
        compiler_params=params(),
        cost_estimate=cost(6 * rows * down.size, [dy, silu, slope, down, pair, out, out, dy]),
        name="hidden_back",
    )(dy, silu, slope, down, pair, pair)


def pair_kernel(left_ref, dgate_ref, dup_ref, act_ref, down_ref, term_ref, out_ref):
    hidden = dgate_ref.shape[1]
    left = left_ref[...]
    term_ref[:, :hidden] = contract(left, dgate_ref[...], ((0,), (0,))).astype(term_ref.dtype)
    term_ref[:, hidden:] = contract(left, dup_ref[...], ((0,), (0,))).astype(term_ref.dtype)
    out_ref[...] = contract(act_ref[...], down_ref[...], ((1,), (1,))).astype(out_ref.dtype)


def pair_terms(left, dgate, dup, act, down):
    rows, columns = left.shape
    hidden = act.shape[1]
    term = jax.ShapeDtypeStruct((columns, 2 * hidden), jnp.bfloat16)
    out = jax.ShapeDtypeStruct((rows, columns), jnp.bfloat16)
    return pl.pallas_call(
        pair_kernel,
        out_shape=(term, out),
        grid=(columns // 512,),
        in_specs=[column_block(left, 512)]
        + [whole_block(a) for a in (dgate, dup, act)]
        + [row_block(down, 512)],
        out_specs=(row_block(term, 512), column_block(out, 512)),
        compiler_params=params(),
        cost_estimate=cost(6 * rows * down.size, [left, dgate, dup, act, down, term, out]),
        name="pair_terms",
    )(left, dgate, dup, act, down)


def weight_kernel(left_ref, *refs):
    left, out_ref = left_ref[...], refs[-1]
    start = 0
    for right_ref in refs[:-1]:
        columns = slice(start, start + right_ref.shape[1])
        out_ref[:, columns] = contract(left, right_ref[...], ((0,), (0,))).astype(out_ref.dtype)
        start = columns.stop


def weight_terms(left, *rights):
    rows, columns = left.shape
    out = jax.ShapeDtypeStruct((columns, sum(r.shape[1] for r in rights)), jnp.bfloat16)
    return pl.pallas_call(
        weight_kernel,
        out_shape=out,
        grid=(columns // 512,),
        in_specs=[column_block(left, 512)] + [whole_block(r) for r in rights],
        out_specs=row_block(out, 512),
        compiler_params=params(),
        cost_estimate=cost(2 * rows * out.size, [left, *rights, out]),
        name="weight_terms",
    )(left, *rights)


def attn_weight_kernel(left_ref, right_ref, left2_ref, right2_ref, out_ref):
    columns = right_ref.shape[1]
    first = contract(left_ref[...], right_ref[...], ((0,), (0,)))
    second = contract(left2_ref[...], right2_ref[...], ((0,), (0,)))
    out_ref[:, :columns] = first.astype(out_ref.dtype)
    out_ref[:, columns:] = second.astype(out_ref.dtype)


def attn_weight_terms(left, right, left2, right2):
    columns = left.shape[1]
    out = jax.ShapeDtypeStruct((columns, right.shape[1] + right2.shape[1]), jnp.bfloat16)
    return pl.pallas_call(
        attn_weight_kernel,
        out_shape=out,
        grid=(columns // 512,),
        in_specs=[
            column_block(left, 512),
            whole_block(right),
            column_block(left2, 512),
            whole_block(right2),
        ],
        out_specs=row_block(out, 512),
        compiler_params=params(),
        cost_estimate=cost(2 * left.shape[0] * out.size, [left, right, left2, right2, out]),
        name="attn_weight_terms",
    )(left, right, left2, right2)


def rotate_back(grad_rows, cosine_table, sine_table):
    half_dim = grad_rows.shape[-1] // 2
    scaled = grad_rows * sine_table
    turned = jnp.concatenate([scaled[..., half_dim:], -scaled[..., :half_dim]], axis=-1)
    return grad_rows * cosine_table + turned


def project_back(left, right):
    return jnp.einsum("rf,df->rd", left, right, preferred_element_type=jnp.float32)


def weight_term(left, right):
    return jnp.einsum("rd,rc->dc", left, right, preferred_element_type=jnp.float32)


def after(value, *earlier):
    return lax.optimization_barrier((value, earlier))[0]


def pick(source, index, axis=0):
    return lax.dynamic_index_in_dim(source, index, axis, keepdims=False)


def swap_tensor(value):
    return lax.ppermute(value, "tensor", [(0, 1), (1, 0)])


def shift_ctx(value, distance=1):
    size = lax.axis_size("ctx")
    return lax.ppermute(value, "ctx", [(i, (i + distance) % size) for i in range(size)])


def swap_x(value):
    return lax.ppermute(value, "dp", [(i, i ^ 1) for i in range(4)])


def swap_y(value):
    return lax.ppermute(value, "dp", [(i, i ^ 2) for i in range(4)])


def ring_blocks(value):
    blocks = [value]
    for _ in range(lax.axis_size("ctx") - 1):
        blocks.append(shift_ctx(blocks[-1]))
    return blocks


def direct_blocks(value):
    return [value] + [shift_ctx(value, d) for d in range(1, lax.axis_size("ctx"))]


def direct_terms(blocks):
    sent = [blocks[j].astype(jnp.bfloat16) for j in range(1, len(blocks))]
    return [blocks[0]] + [shift_ctx(block, -j) for j, block in enumerate(sent, 1)]


def sum_terms(terms):
    total = terms[0].astype(jnp.float32)
    for term in terms[1:]:
        total = total + term.astype(jnp.float32)
    return total


def natural_ctx(blocks):
    size = lax.axis_size("ctx")
    own = lax.axis_index("ctx")
    return jnp.stack([lax.select_n((own - c) % size, *blocks) for c in range(size)])


def spread_ctx(columns):
    size = lax.axis_size("ctx")
    own = lax.axis_index("ctx")
    return [pick(columns, own)] + [
        shift_ctx(pick(columns, (own + distance) % size), distance) for distance in range(1, size)
    ]


def in_order(at, own, other):
    return jnp.stack([jnp.where(at == 0, own, other), jnp.where(at == 0, other, own)])


def gather_near_send(value):
    half = value.shape[0] // 2
    first, second = value[:half], value[half:]
    return first, second, swap_x(first), swap_y(second)


def gather_far_send(first, second, got_x, got_y):
    own = lax.axis_index("dp")
    pair_x = in_order(own % 2, first, got_x)
    pair_y = in_order(own // 2, second, got_y)
    return pair_x, pair_y, swap_y(pair_x), swap_x(pair_y)


def gather_whole(pair_x, pair_y, far_x, far_y):
    own = lax.axis_index("dp")
    full_x = in_order(own // 2, pair_x, far_x)
    full_y = jnp.swapaxes(in_order(own % 2, pair_y, far_y), 0, 1)
    return jnp.stack([full_x, full_y], axis=2).reshape(-1, pair_x.shape[-1])


def add(left, right):
    return (left.astype(jnp.float32) + right.astype(jnp.float32)).astype(jnp.bfloat16)


def scatter_near_send(value):
    rows, columns = value.shape[0] // 4, value.shape[1]
    own = lax.axis_index("dp")
    low, high = own % 2, own // 2
    terms = value.reshape(2, 2, 2, rows // 2, columns)
    first, second = terms[:, :, 0], terms[:, :, 1]
    sent_x, sent_y = pick(first, 1 - low, 1), pick(second, 1 - high, 0)
    return pick(first, low, 1), pick(second, high, 0), swap_x(sent_x), swap_y(sent_y)


def scatter_far_send(kept_x, kept_y, got_x, got_y):
    own = lax.axis_index("dp")
    low, high = own % 2, own // 2
    pair_x, pair_y = add(kept_x, got_x), add(kept_y, got_y)
    far_x, far_y = swap_y(pick(pair_x, 1 - high)), swap_x(pick(pair_y, 1 - low))
    return pick(pair_x, high), pick(pair_y, low), far_x, far_y


def scatter_whole(kept_x, kept_y, far_x, far_y):
    whole = jnp.concatenate([add(kept_x, far_x), add(kept_y, far_y)], axis=0)
    return whole.reshape(lax.axis_size("ctx"), -1, whole.shape[1])


def column_parts(weight, ff_part):
    rows, columns = weight.shape
    size = lax.axis_size("ctx")
    wide = jnp.pad(weight.astype(jnp.bfloat16), ((0, 0), (0, size * ff_part - columns)))
    return jnp.stack([wide[:, c * ff_part : (c + 1) * ff_part] for c in range(size)])


def hidden_grad(parts, columns):
    wide = jnp.concatenate([parts[c] for c in range(parts.shape[0])], axis=1)
    return wide[:, :columns].astype(jnp.float32)


def ctx_terms(parts):
    size = lax.axis_size("ctx")
    own = lax.axis_index("ctx")
    return direct_terms([pick(parts, (own - j) % size) for j in range(size)])


def span_rows(blocks):
    mine = jnp.concatenate([b.reshape(-1, b.shape[-1]) for b in blocks], axis=0)
    return jnp.concatenate([mine, swap_tensor(mine)], axis=0)


def core_sum(term):
    half = term.shape[0] // 2
    other = swap_tensor(term[half:].astype(jnp.bfloat16)).astype(jnp.float32)
    mine = (term[:half].astype(jnp.float32) + other).astype(jnp.bfloat16)
    return list(mine.reshape(lax.axis_size("ctx"), -1, mine.shape[1]))


def sum_everywhere(value):
    for axis in ("dp", "ctx"):
        size, bit = lax.axis_size(axis), 1
        while bit < size:
            value = value + lax.ppermute(value, axis, [(i, i ^ bit) for i in range(size)])
            bit *= 2
    return value


def per_device(
    tokens,
    prefix,
    w_query,
    w_key,
    w_value,
    w_out,
    w_gate,
    w_up,
    w_down,
    b_query,
    b_key,
    b_value,
    norm_attn,
    norm_mlp,
    cotangent,
):
    bf16, f32 = jnp.bfloat16, jnp.float32
    seq_dev, own_rows, model_width = tokens.shape
    ctx_size = lax.axis_size("ctx")
    span_len = own_rows * 2
    seq_len = span_len * ctx_size
    row_count = seq_dev * span_len
    q_cols = w_query.shape[1]
    kv_cols = w_key.shape[1]
    ff_cols = w_gate.shape[1]
    ff_part = -(-ff_cols // (128 * ctx_size)) * 128
    kv_heads = kv_cols // HD
    group_size = q_cols // kv_cols
    score_scale = HD ** (-0.5)
    tensor_at = lax.axis_index("tensor")
    ctx_at = lax.axis_index("ctx")
    own_pos = jnp.arange(own_rows, dtype=jnp.int32)
    in_span = jnp.concatenate([tensor_at * own_rows + own_pos, (1 - tensor_at) * own_rows + own_pos])
    local_pos = ctx_at * span_len + in_span
    key_pos = jnp.concatenate(
        [((ctx_at - j) % ctx_size) * span_len + in_span for j in range(ctx_size)]
    )
    row_pos, col_pos = local_pos[:, None], key_pos[None, :]
    cosine_table, sine_table = rotary_tables(local_pos)
    cosine_flat, sine_flat = cosine_table[:, 0], sine_table[:, 0]
    bias_query = lax.dynamic_slice_in_dim(b_query, tensor_at * q_cols, q_cols)
    bias_key = lax.dynamic_slice_in_dim(b_key, tensor_at * kv_cols, kv_cols)
    bias_value = lax.dynamic_slice_in_dim(b_value, tensor_at * kv_cols, kv_cols)
    bias_all = jnp.concatenate([bias_query, bias_key, bias_value])
    cast_qkv = jnp.concatenate([w.astype(bf16) for w in (w_query, w_key, w_value)], axis=1)
    qkv_blocks = direct_blocks(cast_qkv)
    out_blocks = direct_blocks(after(w_out, qkv_blocks).astype(bf16))
    x_own = tokens.astype(f32)
    attn_root = inverse_root(x_own)
    normed_own = (x_own * attn_root * norm_attn).astype(bf16)
    normed1 = jnp.concatenate([normed_own, swap_tensor(normed_own)], axis=1).reshape(
        row_count, model_width
    )
    qkv_near = gather_near_send(natural_ctx(qkv_blocks).reshape(-1, cast_qkv.shape[1]))
    pair_parts = jnp.concatenate([column_parts(w, ff_part) for w in (w_gate, w_up)], axis=2)
    pair_blocks = spread_ctx(after(pair_parts, out_blocks))
    qkv_far = gather_far_send(*qkv_near)
    full_qkv = gather_whole(*qkv_far)
    out_near = gather_near_send(after(natural_ctx(out_blocks).reshape(-1, q_cols), qkv_far))
    qkv = qkv_heads(
        normed1,
        full_qkv,
        bias_all[None],
        jnp.tile(cosine_flat, (seq_dev, 1)),
        jnp.tile(sine_flat, (seq_dev, 1)),
        (q_cols + kv_cols) // HD,
    )
    queries = qkv[:, :q_cols]
    out_far = gather_far_send(*after(out_near, qkv))
    pair_blocks = after(pair_blocks, qkv)
    kv_sent = qkv[:, q_cols:].reshape(seq_dev, span_len, 2 * kv_cols)
    kv_blocks = direct_blocks(after(kv_sent, pair_blocks, out_near))
    pair_mine = natural_ctx(pair_blocks).reshape(-1, 2 * ff_part)
    kv_blocks = after(kv_blocks, pair_mine)
    out_far = after(out_far, kv_blocks)
    pair_near = gather_near_send(after(pair_mine, out_far))
    kv_rows = jnp.concatenate(kv_blocks, axis=1)
    mixed_low = attend(prefix, row_pos, col_pos, queries, kv_rows)
    full_out = gather_whole(*out_far)
    attn_term = project_back(mixed_low, full_out)
    attn_term = attn_term.reshape(seq_dev, span_len, model_width)
    hidden1 = (
        x_own
        + attn_term[:, :own_rows]
        + swap_tensor(attn_term[:, own_rows:].astype(bf16)).astype(f32)
    )
    mlp_root = inverse_root(hidden1)
    normed2_own = (hidden1 * mlp_root * norm_mlp).astype(bf16)
    normed2_blocks = direct_blocks(normed2_own)
    pair_far = gather_far_send(*after(pair_near, normed2_own))
    normed2 = span_rows(after(normed2_blocks, pair_far[:2]))
    down_blocks = spread_ctx(after(column_parts(w_down, ff_part), normed2))
    down_mine = natural_ctx(down_blocks).reshape(-1, ff_part)
    cotangent_blocks = direct_blocks(after(cotangent, down_blocks))
    pair_far = after(pair_far, down_mine)
    down_near = gather_near_send(after(down_mine, pair_far))
    full_pair = gather_whole(*pair_far)
    activation, silu, slope = hidden_units(normed2, full_pair)
    down_near, cotangent_blocks = after((down_near, cotangent_blocks), activation)
    down_far = gather_far_send(*down_near)
    grad_mlp = span_rows(cotangent_blocks)
    down_term = weight_terms(grad_mlp, after(activation, down_near))
    down_sums = scatter_near_send(down_term)
    full_down = gather_whole(*after(down_far, down_term))
    grad_gate, grad_up, mlp_back = hidden_back(
        after(grad_mlp, down_term), silu, slope, full_down, full_pair
    )
    back_cores = core_sum(mlp_back)
    back_terms = direct_terms(back_cores)
    pair_term, mlp_rows = pair_terms(
        after(normed2, back_cores), grad_gate, grad_up, activation, full_down
    )
    pair_sums = scatter_near_send(pair_term)
    down_sums = scatter_far_send(*after(down_sums, pair_term))
    back_terms = after(back_terms, pair_term)
    mlp_cores = core_sum(after(mlp_rows, pair_term))
    back_terms, down_sums = after((back_terms, down_sums), mlp_cores)
    down_parts = spread_ctx(after(scatter_whole(*down_sums), back_terms))
    grad_normed2 = sum_terms(back_terms).reshape(tokens.shape)
    grad_out = cotangent.astype(f32)
    scaled2 = norm_mlp * grad_normed2
    grad_hidden1 = (
        grad_out
        + mlp_root * scaled2
        - hidden1 * mlp_root**3 * jnp.mean(scaled2 * hidden1, axis=-1, keepdims=True)
    )
    gain_mlp = jnp.sum(grad_normed2 * hidden1 * mlp_root, axis=(0, 1))
    grad_own = grad_hidden1.astype(bf16)
    grad_attn = jnp.concatenate([grad_own, swap_tensor(grad_own)], axis=1).reshape(
        row_count, model_width
    )
    grad_mixed = jnp.dot(grad_attn, full_out, preferred_element_type=f32).astype(bf16)
    grad_q, kv_terms = attend_back(
        prefix, row_pos, col_pos, queries, kv_rows, grad_mixed, cosine_flat, sine_flat
    )
    down_parts = after(down_parts, kv_terms)
    kv_sent = after(kv_terms, down_parts)
    pair_sums = scatter_far_send(*after(pair_sums, kv_sent))
    kv_own = direct_terms(
        [kv_sent[:, j * span_len : (j + 1) * span_len] for j in range(ctx_size)]
    )
    mlp_terms = direct_terms(after(mlp_cores, kv_own))
    kv_sum = sum_terms(kv_own)
    grad_k = rotate_back(kv_sum[:, :, None, :kv_cols], cosine_table, sine_table)
    grad_k = grad_k.reshape(row_count, kv_cols).astype(bf16)
    grad_v = kv_sum[:, :, kv_cols:].reshape(row_count, kv_cols).astype(bf16)
    grad_qkv = jnp.concatenate([grad_q, grad_k, grad_v], axis=1)
    attn_term = attn_weight_terms(normed1, after(grad_qkv, pair_sums), grad_attn, mixed_low)
    attn_sums = scatter_near_send(attn_term)
    mlp_terms = after(mlp_terms, attn_term)
    grad_w_down = hidden_grad(natural_ctx(down_parts), ff_cols)
    attn_back = project_back(grad_qkv, full_qkv).reshape(seq_dev, span_len, model_width)
    grad_normed1 = attn_back[:, :own_rows] + swap_tensor(
        attn_back[:, own_rows:].astype(bf16)
    ).astype(f32)
    scaled1 = norm_attn * grad_normed1
    grad_tokens = (
        grad_hidden1
        + attn_root * scaled1
        - x_own * attn_root**3 * jnp.mean(scaled1 * x_own, axis=-1, keepdims=True)
    ).astype(bf16)
    attn_sums = scatter_far_send(*after(attn_sums, grad_tokens))
    output = (hidden1 + sum_terms(mlp_terms).reshape(tokens.shape)).astype(bf16)
    pair_grads = spread_ctx(after(scatter_whole(*pair_sums), mlp_terms, attn_sums[:2]))
    gain_attn = jnp.sum(grad_normed1 * x_own * attn_root, axis=(0, 1))
    place_query = lax.dynamic_update_slice_in_dim(
        jnp.zeros_like(b_query), jnp.sum(grad_q, axis=0, dtype=f32), tensor_at * q_cols, 0
    )
    place_key = lax.dynamic_update_slice_in_dim(
        jnp.zeros_like(b_key), jnp.sum(grad_k, axis=0, dtype=f32), tensor_at * kv_cols, 0
    )
    place_value = lax.dynamic_update_slice_in_dim(
        jnp.zeros_like(b_value), jnp.sum(grad_v, axis=0, dtype=f32), tensor_at * kv_cols, 0
    )
    sums = jnp.concatenate([gain_attn, gain_mlp, place_query, place_key, place_value])
    attn_terms = ctx_terms(scatter_whole(*after(attn_sums, pair_grads[1])))
    sums = after(sums, pair_grads[1]).reshape(-1, 128)
    sums = sum_everywhere(sums + swap_tensor(sums)).reshape(-1)
    splits = [model_width, 2 * model_width]
    splits += [splits[1] + b_query.shape[0], splits[1] + b_query.shape[0] + b_key.shape[0]]
    sum_attn, sum_mlp, sum_query, sum_key, sum_value = jnp.split(sums, splits)
    attn_grads = sum_terms(attn_terms)
    grad_w_qkv, grad_w_out = attn_grads[:, :-q_cols], attn_grads[:, -q_cols:]
    pair_grads = natural_ctx(pair_grads)
    grad_w_gate = hidden_grad(pair_grads[:, :, :ff_part], ff_cols)
    grad_w_up = hidden_grad(pair_grads[:, :, ff_part:], ff_cols)
    grad_w_query = grad_w_qkv[:, :q_cols]
    grad_w_key = grad_w_qkv[:, q_cols : q_cols + kv_cols]
    grad_w_value = grad_w_qkv[:, q_cols + kv_cols :]
    return (
        output,
        grad_tokens,
        grad_w_query,
        grad_w_key,
        grad_w_value,
        grad_w_out,
        grad_w_gate,
        grad_w_up,
        grad_w_down,
        sum_query,
        sum_key,
        sum_value,
        sum_attn,
        sum_mlp,
    )


def solution(mesh):
    placed = (
        P("dp", ("ctx", "tensor"), None),
        P("dp"),
        P(("dp", "ctx"), "tensor"),
        P(("dp", "ctx"), "tensor"),
        P(("dp", "ctx"), "tensor"),
        P(("dp", "ctx"), "tensor"),
        P(("dp", "ctx"), "tensor"),
        P(("dp", "ctx"), "tensor"),
        P(("dp", "ctx"), "tensor"),
        P(),
        P(),
        P(),
        P(),
        P(),
        P("dp", ("ctx", "tensor"), None),
    )
    return jax.shard_map(
        per_device,
        mesh=mesh,
        in_specs=placed,
        out_specs=(
            P("dp", ("ctx", "tensor"), None),
            P("dp", ("ctx", "tensor"), None),
            P(("dp", "ctx"), "tensor"),
            P(("dp", "ctx"), "tensor"),
            P(("dp", "ctx"), "tensor"),
            P(("dp", "ctx"), "tensor"),
            P(("dp", "ctx"), "tensor"),
            P(("dp", "ctx"), "tensor"),
            P(("dp", "ctx"), "tensor"),
            P(),
            P(),
            P(),
            P(),
            P(),
        ),
        check_vma=False,
    )
```

```python
import functools

import jax
import jax.numpy as jnp
from jax import lax
from jax.experimental import pallas as pl
from jax.experimental.pallas import tpu as pltpu
from jax.sharding import PartitionSpec as P

HD = 128


epsilon = 1e-06
rope_base = 1000000.0


def inverse_root(value):
    return lax.rsqrt(jnp.mean(value * value, axis=-1, keepdims=True) + epsilon)


def rotary_tables(positions):
    half_dim = HD // 2
    frequency = rope_base ** (-2.0 * jnp.arange(half_dim, dtype=jnp.float32) / HD)
    angles = positions.astype(jnp.float32)[:, None] * frequency[None, :]
    angles = jnp.concatenate([angles, angles], axis=1)
    return (jnp.cos(angles)[:, None, :], jnp.sin(angles)[:, None, :])


VMEM_LIMIT = 28 * 1024 * 1024


def params():
    return pltpu.CompilerParams(vmem_limit_bytes=VMEM_LIMIT)


def cost(flops, arrays):
    moved = sum(a.size * a.dtype.itemsize for a in arrays)
    return pl.CostEstimate(flops=flops, bytes_accessed=moved, transcendentals=0)


def contract(left, right, dims):
    return lax.dot_general(left, right, (dims, ((), ())), preferred_element_type=jnp.float32)


def half_sign(shape):
    return jnp.where(lax.broadcasted_iota(jnp.int32, shape, 1) < shape[1] // 2, 1.0, -1.0)


def qkv_kernel(rope_heads, x_ref, w_ref, b_ref, cos_ref, sin_ref, out_ref):
    at = pl.program_id(0)
    heads = w_ref.shape[1] // HD
    total = contract(x_ref[...], w_ref[...], ((1,), (0,))) + b_ref[...]
    cosine, sine = cos_ref[...], sin_ref[...]
    signed = -half_sign(sine.shape) * sine
    for head in range(heads):
        value = total[:, head * HD : (head + 1) * HD]
        turned = value * cosine + pltpu.roll(value, HD // 2, 1) * signed
        kept = jnp.where(at * heads + head < rope_heads, turned, value)
        out_ref[:, head * HD : (head + 1) * HD] = kept.astype(out_ref.dtype)


def qkv_heads(x, weight, bias, cosine, sine, rope_heads):
    rows, columns = x.shape[0], weight.shape[1]
    out = jax.ShapeDtypeStruct((rows, columns), jnp.bfloat16)
    whole = lambda a: pl.BlockSpec(a.shape, lambda i: (0, 0))
    return pl.pallas_call(
        functools.partial(qkv_kernel, rope_heads),
        out_shape=out,
        grid=(columns // 256,),
        in_specs=[
            whole(x),
            pl.BlockSpec((weight.shape[0], 256), lambda i: (0, i)),
            pl.BlockSpec((1, 256), lambda i: (0, i)),
            whole(cosine),
            whole(sine),
        ],
        out_specs=pl.BlockSpec((rows, 256), lambda i: (0, i)),
        compiler_params=params(),
        cost_estimate=cost(2 * x.size * columns, [x, weight, out]),
        name="qkv_heads",
    )(x, weight, bias, cosine, sine)


def probabilities_of(query, keys, allowed):
    scores = contract(query, keys, ((1,), (1,))) * HD ** (-0.5)
    scores = jnp.where(allowed, scores, -1e30)
    weights = jnp.exp(scores - jnp.max(scores, axis=-1, keepdims=True))
    return weights / jnp.sum(weights, axis=-1, keepdims=True)


def allowed_of(prefix_ref, row_ref, key_ref):
    keys = key_ref[...]
    return (keys <= row_ref[...]) | (keys < prefix_ref[pl.program_id(0)])


def attend_kernel(prefix_ref, row_ref, key_ref, q_ref, kv_ref, out_ref):
    allowed = allowed_of(prefix_ref, row_ref, key_ref)
    keys, values = kv_ref[0, :, :HD], kv_ref[0, :, HD:]
    for head in range(q_ref.shape[1] // HD):
        columns = slice(head * HD, (head + 1) * HD)
        chances = probabilities_of(q_ref[:, columns], keys, allowed).astype(jnp.bfloat16)
        out_ref[:, columns] = contract(chances, values, ((1,), (0,))).astype(out_ref.dtype)


def attend_back_kernel(
    prefix_ref, row_ref, key_ref, q_ref, kv_ref, grad_ref, cos_ref, sin_ref, dq_ref, dkv_ref
):
    allowed = allowed_of(prefix_ref, row_ref, key_ref)
    keys, values = kv_ref[0, :, :HD], kv_ref[0, :, HD:]
    sign = half_sign(cos_ref.shape)
    scale = HD ** (-0.5)
    grad_keys = jnp.zeros(keys.shape, jnp.float32)
    grad_values = jnp.zeros(keys.shape, jnp.float32)
    for head in range(q_ref.shape[1] // HD):
        columns = slice(head * HD, (head + 1) * HD)
        query, grad = q_ref[:, columns], grad_ref[:, columns]
        chances = probabilities_of(query, keys, allowed)
        rounded = chances.astype(jnp.bfloat16)
        grad_chances = contract(grad, values, ((1,), (1,)))
        offset = jnp.sum(rounded.astype(jnp.float32) * grad_chances, axis=-1, keepdims=True)
        grad_scores = (chances * (grad_chances - offset)).astype(jnp.bfloat16)
        turned = contract(grad_scores, keys, ((1,), (0,))) * scale
        back = turned * cos_ref[...] + pltpu.roll(turned * sin_ref[...], HD // 2, 1) * sign
        dq_ref[:, columns] = back.astype(dq_ref.dtype)
        grad_keys += contract(grad_scores, query, ((0,), (0,)))
        grad_values += contract(rounded, grad, ((0,), (0,)))
    dkv_ref[0, :, :HD] = (grad_keys * scale).astype(dkv_ref.dtype)
    dkv_ref[0, :, HD:] = grad_values.astype(dkv_ref.dtype)


def attention_specs(query, kv, row_pos, key_pos):
    rows = query.shape[0] // kv.shape[0]
    heads = pl.BlockSpec((rows, query.shape[1]), lambda i: (i, 0))
    both = pl.BlockSpec((1,) + kv.shape[1:], lambda i: (i, 0, 0))
    return heads, [
        pl.BlockSpec(memory_space=pltpu.SMEM),
        pl.BlockSpec(row_pos.shape, lambda i: (0, 0)),
        pl.BlockSpec(key_pos.shape, lambda i: (0, 0)),
        heads,
        both,
    ], both


def attend(prefix, row_pos, key_pos, query, kv):
    heads, specs, _ = attention_specs(query, kv, row_pos, key_pos)
    return pl.pallas_call(
        attend_kernel,
        out_shape=jax.ShapeDtypeStruct(query.shape, jnp.bfloat16),
        grid=(kv.shape[0],),
        in_specs=specs,
        out_specs=heads,
        compiler_params=params(),
        cost_estimate=cost(4 * query.size * kv.shape[1], [query, kv, query]),
        name="attend",
    )(prefix, row_pos, key_pos, query, kv)


def attend_back(prefix, row_pos, key_pos, query, kv, grad, cosine, sine):
    heads, specs, both = attention_specs(query, kv, row_pos, key_pos)
    table = pl.BlockSpec(cosine.shape, lambda i: (0, 0))
    return pl.pallas_call(
        attend_back_kernel,
        out_shape=(
            jax.ShapeDtypeStruct(query.shape, jnp.bfloat16),
            jax.ShapeDtypeStruct(kv.shape, jnp.bfloat16),
        ),
        grid=(kv.shape[0],),
        in_specs=specs + [heads, table, table],
        out_specs=(heads, both),
        compiler_params=params(),
        cost_estimate=cost(10 * query.size * kv.shape[1], [query, kv, grad, query, kv]),
        name="attend_back",
    )(prefix, row_pos, key_pos, query, kv, grad, cosine, sine)


STEP = 384
ROWS = 1024


def whole_block(array):
    return pl.BlockSpec(array.shape, lambda i: (0, 0))


def column_block(array, columns):
    return pl.BlockSpec((array.shape[0], columns), lambda i: (0, i))


def row_block(array, rows):
    return pl.BlockSpec((rows, array.shape[1]), lambda i: (i, 0))


def hidden_kernel(x_ref, gate_ref, up_ref, act_ref, silu_ref, slope_ref):
    x = x_ref[...]
    gate = contract(x, gate_ref[...], ((1,), (0,)))
    up = contract(x, up_ref[...], ((1,), (0,)))
    sigmoid = jax.nn.sigmoid(gate)
    silu = gate * sigmoid
    act_ref[...] = (silu * up).astype(act_ref.dtype)
    silu_ref[...] = silu.astype(silu_ref.dtype)
    slope_ref[...] = (up * sigmoid * (1.0 + gate * (1.0 - sigmoid))).astype(slope_ref.dtype)


def row_tile(array):
    return pl.BlockSpec((ROWS, array.shape[1]), lambda i, j: (i, 0))


def both_tile():
    return pl.BlockSpec((ROWS, STEP), lambda i, j: (i, j))


def column_tile(array, offset=0):
    return pl.BlockSpec((array.shape[0], STEP), lambda i, j: (0, j + offset))


def hidden_units(x, pair):
    rows, hidden = x.shape[0], pair.shape[1] // 2
    out = jax.ShapeDtypeStruct((rows, hidden), jnp.bfloat16)
    return pl.pallas_call(
        hidden_kernel,
        out_shape=(out, out, out),
        grid=(rows // ROWS, hidden // STEP),
        in_specs=[row_tile(x), column_tile(pair), column_tile(pair, hidden // STEP)],
        out_specs=(both_tile(),) * 3,
        compiler_params=params(),
        cost_estimate=cost(2 * rows * pair.size, [x, pair, out, out, out]),
        name="hidden_units",
    )(x, pair, pair)


def hidden_back_kernel(
    dy_ref, silu_ref, slope_ref, down_ref, gate_ref, up_ref, dgate_ref, dup_ref, dx_ref, total_ref
):
    grad = contract(dy_ref[...], down_ref[...], ((1,), (0,)))
    dup = (grad * silu_ref[...].astype(jnp.float32)).astype(jnp.bfloat16)
    dgate = (grad * slope_ref[...].astype(jnp.float32)).astype(jnp.bfloat16)
    dup_ref[...] = dup
    dgate_ref[...] = dgate
    both = jnp.concatenate([dgate, dup], axis=1)
    weights = jnp.concatenate([gate_ref[...], up_ref[...]], axis=1)
    at, last = pl.program_id(1), pl.num_programs(1) - 1
    term = contract(both, weights, ((1,), (1,)))

    @pl.when(at == 0)
    def _():
        total_ref[...] = term

    @pl.when((at > 0) & (at < last))
    def _():
        total_ref[...] += term

    @pl.when((at > 0) & (at == last))
    def _():
        dx_ref[...] = (total_ref[...] + term).astype(dx_ref.dtype)

    @pl.when((at == 0) & (at == last))
    def _():
        dx_ref[...] = term.astype(dx_ref.dtype)


def hidden_back(dy, silu, slope, down, pair):
    rows, hidden = silu.shape
    out = jax.ShapeDtypeStruct((rows, hidden), jnp.bfloat16)
    out_x = jax.ShapeDtypeStruct(dy.shape, jnp.bfloat16)
    tile = both_tile()
    return pl.pallas_call(
        hidden_back_kernel,
        out_shape=(out, out, out_x),
        grid=(rows // ROWS, hidden // STEP),
        in_specs=[
            row_tile(dy),
            tile,
            tile,
            column_tile(down),
            column_tile(pair),
            column_tile(pair, hidden // STEP),
        ],
        out_specs=(tile, tile, row_tile(dy)),
        scratch_shapes=[pltpu.VMEM((ROWS, dy.shape[1]), jnp.float32)],
        compiler_params=params(),
        cost_estimate=cost(6 * rows * down.size, [dy, silu, slope, down, pair, out, out, dy]),
        name="hidden_back",
    )(dy, silu, slope, down, pair, pair)


def pair_kernel(left_ref, dgate_ref, dup_ref, act_ref, down_ref, term_ref, out_ref):
    hidden = dgate_ref.shape[1]
    left = left_ref[...]
    term_ref[:, :hidden] = contract(left, dgate_ref[...], ((0,), (0,))).astype(term_ref.dtype)
    term_ref[:, hidden:] = contract(left, dup_ref[...], ((0,), (0,))).astype(term_ref.dtype)
    out_ref[...] = contract(act_ref[...], down_ref[...], ((1,), (1,))).astype(out_ref.dtype)


def pair_terms(left, dgate, dup, act, down):
    rows, columns = left.shape
    hidden = act.shape[1]
    term = jax.ShapeDtypeStruct((columns, 2 * hidden), jnp.bfloat16)
    out = jax.ShapeDtypeStruct((rows, columns), jnp.bfloat16)
    return pl.pallas_call(
        pair_kernel,
        out_shape=(term, out),
        grid=(columns // 512,),
        in_specs=[column_block(left, 512)]
        + [whole_block(a) for a in (dgate, dup, act)]
        + [row_block(down, 512)],
        out_specs=(row_block(term, 512), column_block(out, 512)),
        compiler_params=params(),
        cost_estimate=cost(6 * rows * down.size, [left, dgate, dup, act, down, term, out]),
        name="pair_terms",
    )(left, dgate, dup, act, down)


def weight_kernel(left_ref, *refs):
    left, out_ref = left_ref[...], refs[-1]
    start = 0
    for right_ref in refs[:-1]:
        columns = slice(start, start + right_ref.shape[1])
        out_ref[:, columns] = contract(left, right_ref[...], ((0,), (0,))).astype(out_ref.dtype)
        start = columns.stop


def weight_terms(left, *rights):
    rows, columns = left.shape
    out = jax.ShapeDtypeStruct((columns, sum(r.shape[1] for r in rights)), jnp.bfloat16)
    return pl.pallas_call(
        weight_kernel,
        out_shape=out,
        grid=(columns // 512,),
        in_specs=[column_block(left, 512)] + [whole_block(r) for r in rights],
        out_specs=row_block(out, 512),
        compiler_params=params(),
        cost_estimate=cost(2 * rows * out.size, [left, *rights, out]),
        name="weight_terms",
    )(left, *rights)


def attn_weight_kernel(left_ref, right_ref, left2_ref, right2_ref, out_ref):
    columns = right_ref.shape[1]
    first = contract(left_ref[...], right_ref[...], ((0,), (0,)))
    second = contract(left2_ref[...], right2_ref[...], ((0,), (0,)))
    out_ref[:, :columns] = first.astype(out_ref.dtype)
    out_ref[:, columns:] = second.astype(out_ref.dtype)


def attn_weight_terms(left, right, left2, right2):
    columns = left.shape[1]
    out = jax.ShapeDtypeStruct((columns, right.shape[1] + right2.shape[1]), jnp.bfloat16)
    return pl.pallas_call(
        attn_weight_kernel,
        out_shape=out,
        grid=(columns // 512,),
        in_specs=[
            column_block(left, 512),
            whole_block(right),
            column_block(left2, 512),
            whole_block(right2),
        ],
        out_specs=row_block(out, 512),
        compiler_params=params(),
        cost_estimate=cost(2 * left.shape[0] * out.size, [left, right, left2, right2, out]),
        name="attn_weight_terms",
    )(left, right, left2, right2)


def rotate_back(grad_rows, cosine_table, sine_table):
    half_dim = grad_rows.shape[-1] // 2
    scaled = grad_rows * sine_table
    turned = jnp.concatenate([scaled[..., half_dim:], -scaled[..., :half_dim]], axis=-1)
    return grad_rows * cosine_table + turned


def project_back(left, right):
    return jnp.einsum("rf,df->rd", left, right, preferred_element_type=jnp.float32)


def weight_term(left, right):
    return jnp.einsum("rd,rc->dc", left, right, preferred_element_type=jnp.float32)


def after(value, *earlier):
    return lax.optimization_barrier((value, earlier))[0]


def pick(source, index, axis=0):
    return lax.dynamic_index_in_dim(source, index, axis, keepdims=False)


def swap_tensor(value):
    return lax.ppermute(value, "tensor", [(0, 1), (1, 0)])


def shift_ctx(value, distance=1):
    size = lax.axis_size("ctx")
    return lax.ppermute(value, "ctx", [(i, (i + distance) % size) for i in range(size)])


def swap_x(value):
    return lax.ppermute(value, "dp", [(i, i ^ 1) for i in range(4)])


def swap_y(value):
    return lax.ppermute(value, "dp", [(i, i ^ 2) for i in range(4)])


def ring_blocks(value):
    blocks = [value]
    for _ in range(lax.axis_size("ctx") - 1):
        blocks.append(shift_ctx(blocks[-1]))
    return blocks


def direct_blocks(value):
    return [value] + [shift_ctx(value, d) for d in range(1, lax.axis_size("ctx"))]


def direct_terms(blocks):
    sent = [blocks[j].astype(jnp.bfloat16) for j in range(1, len(blocks))]
    return [blocks[0]] + [shift_ctx(block, -j) for j, block in enumerate(sent, 1)]


def sum_terms(terms):
    total = terms[0].astype(jnp.float32)
    for term in terms[1:]:
        total = total + term.astype(jnp.float32)
    return total


def natural_ctx(blocks):
    size = lax.axis_size("ctx")
    own = lax.axis_index("ctx")
    return jnp.stack([lax.select_n((own - c) % size, *blocks) for c in range(size)])


def spread_ctx(columns):
    size = lax.axis_size("ctx")
    own = lax.axis_index("ctx")
    return [pick(columns, own)] + [
        shift_ctx(pick(columns, (own + distance) % size), distance) for distance in range(1, size)
    ]


def in_order(at, own, other):
    return jnp.stack([jnp.where(at == 0, own, other), jnp.where(at == 0, other, own)])


def gather_near_send(value):
    half = value.shape[0] // 2
    first, second = value[:half], value[half:]
    return first, second, swap_x(first), swap_y(second)


def gather_far_send(first, second, got_x, got_y):
    own = lax.axis_index("dp")
    pair_x = in_order(own % 2, first, got_x)
    pair_y = in_order(own // 2, second, got_y)
    return pair_x, pair_y, swap_y(pair_x), swap_x(pair_y)


def gather_whole(pair_x, pair_y, far_x, far_y):
    own = lax.axis_index("dp")
    full_x = in_order(own // 2, pair_x, far_x)
    full_y = jnp.swapaxes(in_order(own % 2, pair_y, far_y), 0, 1)
    return jnp.stack([full_x, full_y], axis=2).reshape(-1, pair_x.shape[-1])


def add(left, right):
    return (left.astype(jnp.float32) + right.astype(jnp.float32)).astype(jnp.bfloat16)


def scatter_near_send(value):
    rows, columns = value.shape[0] // 4, value.shape[1]
    own = lax.axis_index("dp")
    low, high = own % 2, own // 2
    terms = value.reshape(2, 2, 2, rows // 2, columns)
    first, second = terms[:, :, 0], terms[:, :, 1]
    sent_x, sent_y = pick(first, 1 - low, 1), pick(second, 1 - high, 0)
    return pick(first, low, 1), pick(second, high, 0), swap_x(sent_x), swap_y(sent_y)


def scatter_far_send(kept_x, kept_y, got_x, got_y):
    own = lax.axis_index("dp")
    low, high = own % 2, own // 2
    pair_x, pair_y = add(kept_x, got_x), add(kept_y, got_y)
    far_x, far_y = swap_y(pick(pair_x, 1 - high)), swap_x(pick(pair_y, 1 - low))
    return pick(pair_x, high), pick(pair_y, low), far_x, far_y


def scatter_whole(kept_x, kept_y, far_x, far_y):
    whole = jnp.concatenate([add(kept_x, far_x), add(kept_y, far_y)], axis=0)
    return whole.reshape(lax.axis_size("ctx"), -1, whole.shape[1])


def column_parts(weight, ff_part):
    rows, columns = weight.shape
    size = lax.axis_size("ctx")
    wide = jnp.pad(weight.astype(jnp.bfloat16), ((0, 0), (0, size * ff_part - columns)))
    return jnp.stack([wide[:, c * ff_part : (c + 1) * ff_part] for c in range(size)])


def hidden_grad(parts, columns):
    wide = jnp.concatenate([parts[c] for c in range(parts.shape[0])], axis=1)
    return wide[:, :columns].astype(jnp.float32)


def ctx_terms(parts):
    size = lax.axis_size("ctx")
    own = lax.axis_index("ctx")
    return direct_terms([pick(parts, (own - j) % size) for j in range(size)])


def span_rows(blocks):
    mine = jnp.concatenate([b.reshape(-1, b.shape[-1]) for b in blocks], axis=0)
    return jnp.concatenate([mine, swap_tensor(mine)], axis=0)


def core_sum(term):
    half = term.shape[0] // 2
    other = swap_tensor(term[half:].astype(jnp.bfloat16)).astype(jnp.float32)
    mine = (term[:half].astype(jnp.float32) + other).astype(jnp.bfloat16)
    return list(mine.reshape(lax.axis_size("ctx"), -1, mine.shape[1]))


def sum_everywhere(value):
    for axis in ("dp", "ctx"):
        size, bit = lax.axis_size(axis), 1
        while bit < size:
            value = value + lax.ppermute(value, axis, [(i, i ^ bit) for i in range(size)])
            bit *= 2
    return value


def per_device(
    tokens,
    prefix,
    w_query,
    w_key,
    w_value,
    w_out,
    w_gate,
    w_up,
    w_down,
    b_query,
    b_key,
    b_value,
    norm_attn,
    norm_mlp,
    cotangent,
):
    bf16, f32 = jnp.bfloat16, jnp.float32
    seq_dev, own_rows, model_width = tokens.shape
    ctx_size = lax.axis_size("ctx")
    span_len = own_rows * 2
    seq_len = span_len * ctx_size
    row_count = seq_dev * span_len
    q_cols = w_query.shape[1]
    kv_cols = w_key.shape[1]
    ff_cols = w_gate.shape[1]
    ff_part = -(-ff_cols // (128 * ctx_size)) * 128
    kv_heads = kv_cols // HD
    group_size = q_cols // kv_cols
    score_scale = HD ** (-0.5)
    tensor_at = lax.axis_index("tensor")
    ctx_at = lax.axis_index("ctx")
    own_pos = jnp.arange(own_rows, dtype=jnp.int32)
    in_span = jnp.concatenate([tensor_at * own_rows + own_pos, (1 - tensor_at) * own_rows + own_pos])
    local_pos = ctx_at * span_len + in_span
    key_pos = jnp.concatenate(
        [((ctx_at - j) % ctx_size) * span_len + in_span for j in range(ctx_size)]
    )
    row_pos, col_pos = local_pos[:, None], key_pos[None, :]
    cosine_table, sine_table = rotary_tables(local_pos)
    cosine_flat, sine_flat = cosine_table[:, 0], sine_table[:, 0]
    bias_query = lax.dynamic_slice_in_dim(b_query, tensor_at * q_cols, q_cols)
    bias_key = lax.dynamic_slice_in_dim(b_key, tensor_at * kv_cols, kv_cols)
    bias_value = lax.dynamic_slice_in_dim(b_value, tensor_at * kv_cols, kv_cols)
    bias_all = jnp.concatenate([bias_query, bias_key, bias_value])
    cast_qkv = jnp.concatenate([w.astype(bf16) for w in (w_query, w_key, w_value)], axis=1)
    qkv_blocks = direct_blocks(cast_qkv)
    out_blocks = direct_blocks(after(w_out, qkv_blocks).astype(bf16))
    x_own = tokens.astype(f32)
    attn_root = inverse_root(x_own)
    normed_own = (x_own * attn_root * norm_attn).astype(bf16)
    normed1 = jnp.concatenate([normed_own, swap_tensor(normed_own)], axis=1).reshape(
        row_count, model_width
    )
    qkv_near = gather_near_send(natural_ctx(qkv_blocks).reshape(-1, cast_qkv.shape[1]))
    pair_parts = jnp.concatenate([column_parts(w, ff_part) for w in (w_gate, w_up)], axis=2)
    pair_blocks = spread_ctx(after(pair_parts, out_blocks))
    qkv_far = gather_far_send(*qkv_near)
    full_qkv = gather_whole(*qkv_far)
    out_near = gather_near_send(after(natural_ctx(out_blocks).reshape(-1, q_cols), qkv_far))
    qkv = qkv_heads(
        normed1,
        full_qkv,
        bias_all[None],
        jnp.tile(cosine_flat, (seq_dev, 1)),
        jnp.tile(sine_flat, (seq_dev, 1)),
        (q_cols + kv_cols) // HD,
    )
    queries = qkv[:, :q_cols]
    out_far = gather_far_send(*after(out_near, qkv))
    pair_blocks = after(pair_blocks, qkv)
    kv_sent = qkv[:, q_cols:].reshape(seq_dev, span_len, 2 * kv_cols)
    kv_blocks = direct_blocks(after(kv_sent, pair_blocks, out_near))
    pair_mine = natural_ctx(pair_blocks).reshape(-1, 2 * ff_part)
    kv_blocks = after(kv_blocks, pair_mine)
    out_far = after(out_far, kv_blocks)
    pair_near = gather_near_send(after(pair_mine, out_far))
    kv_rows = jnp.concatenate(kv_blocks, axis=1)
    mixed_low = attend(prefix, row_pos, col_pos, queries, kv_rows)
    full_out = gather_whole(*out_far)
    attn_term = project_back(mixed_low, full_out)
    attn_term = attn_term.reshape(seq_dev, span_len, model_width)
    hidden1 = (
        x_own
        + attn_term[:, :own_rows]
        + swap_tensor(attn_term[:, own_rows:].astype(bf16)).astype(f32)
    )
    mlp_root = inverse_root(hidden1)
    normed2_own = (hidden1 * mlp_root * norm_mlp).astype(bf16)
    normed2_blocks = direct_blocks(normed2_own)
    pair_far = gather_far_send(*after(pair_near, normed2_own))
    normed2 = span_rows(after(normed2_blocks, pair_far[:2]))
    down_blocks = spread_ctx(after(column_parts(w_down, ff_part), normed2))
    down_mine = natural_ctx(down_blocks).reshape(-1, ff_part)
    cotangent_blocks = direct_blocks(after(cotangent, down_blocks))
    pair_far = after(pair_far, down_mine)
    down_near = gather_near_send(after(down_mine, pair_far))
    full_pair = gather_whole(*pair_far)
    activation, silu, slope = hidden_units(normed2, full_pair)
    down_near, cotangent_blocks = after((down_near, cotangent_blocks), activation)
    down_far = gather_far_send(*down_near)
    grad_mlp = span_rows(cotangent_blocks)
    down_term = weight_terms(grad_mlp, after(activation, down_near))
    down_sums = scatter_near_send(down_term)
    full_down = gather_whole(*after(down_far, down_term))
    grad_gate, grad_up, mlp_back = hidden_back(
        after(grad_mlp, down_term), silu, slope, full_down, full_pair
    )
    back_cores = core_sum(mlp_back)
    back_terms = direct_terms(back_cores)
    pair_term, mlp_rows = pair_terms(
        after(normed2, back_cores), grad_gate, grad_up, activation, full_down
    )
    pair_sums = scatter_near_send(pair_term)
    down_sums = scatter_far_send(*after(down_sums, pair_term))
    back_terms = after(back_terms, pair_term)
    mlp_cores = core_sum(after(mlp_rows, pair_term))
    back_terms, down_sums = after((back_terms, down_sums), mlp_cores)
    down_parts = spread_ctx(after(scatter_whole(*down_sums), back_terms))
    grad_normed2 = sum_terms(back_terms).reshape(tokens.shape)
    grad_out = cotangent.astype(f32)
    scaled2 = norm_mlp * grad_normed2
    grad_hidden1 = (
        grad_out
        + mlp_root * scaled2
        - hidden1 * mlp_root**3 * jnp.mean(scaled2 * hidden1, axis=-1, keepdims=True)
    )
    gain_mlp = jnp.sum(grad_normed2 * hidden1 * mlp_root, axis=(0, 1))
    grad_own = grad_hidden1.astype(bf16)
    grad_attn = jnp.concatenate([grad_own, swap_tensor(grad_own)], axis=1).reshape(
        row_count, model_width
    )
    grad_mixed = jnp.dot(grad_attn, full_out, preferred_element_type=f32).astype(bf16)
    grad_q, kv_terms = attend_back(
        prefix, row_pos, col_pos, queries, kv_rows, grad_mixed, cosine_flat, sine_flat
    )
    down_parts = after(down_parts, kv_terms)
    kv_sent = after(kv_terms, down_parts)
    pair_sums = scatter_far_send(*after(pair_sums, kv_sent))
    kv_own = direct_terms(
        [kv_sent[:, j * span_len : (j + 1) * span_len] for j in range(ctx_size)]
    )
    mlp_terms = direct_terms(after(mlp_cores, kv_own))
    kv_sum = sum_terms(kv_own)
    grad_k = rotate_back(kv_sum[:, :, None, :kv_cols], cosine_table, sine_table)
    grad_k = grad_k.reshape(row_count, kv_cols).astype(bf16)
    grad_v = kv_sum[:, :, kv_cols:].reshape(row_count, kv_cols).astype(bf16)
    grad_qkv = jnp.concatenate([grad_q, grad_k, grad_v], axis=1)
    attn_term = attn_weight_terms(normed1, after(grad_qkv, pair_sums), grad_attn, mixed_low)
    attn_sums = scatter_near_send(attn_term)
    mlp_terms = after(mlp_terms, attn_term)
    grad_w_down = hidden_grad(natural_ctx(down_parts), ff_cols)
    attn_back = project_back(grad_qkv, full_qkv).reshape(seq_dev, span_len, model_width)
    grad_normed1 = attn_back[:, :own_rows] + swap_tensor(
        attn_back[:, own_rows:].astype(bf16)
    ).astype(f32)
    scaled1 = norm_attn * grad_normed1
    grad_tokens = (
        grad_hidden1
        + attn_root * scaled1
        - x_own * attn_root**3 * jnp.mean(scaled1 * x_own, axis=-1, keepdims=True)
    ).astype(bf16)
    attn_sums = scatter_far_send(*after(attn_sums, grad_tokens))
    output = (hidden1 + sum_terms(mlp_terms).reshape(tokens.shape)).astype(bf16)
    pair_grads = spread_ctx(after(scatter_whole(*pair_sums), mlp_terms, attn_sums[:2]))
    gain_attn = jnp.sum(grad_normed1 * x_own * attn_root, axis=(0, 1))
    place_query = lax.dynamic_update_slice_in_dim(
        jnp.zeros_like(b_query), jnp.sum(grad_q, axis=0, dtype=f32), tensor_at * q_cols, 0
    )
    place_key = lax.dynamic_update_slice_in_dim(
        jnp.zeros_like(b_key), jnp.sum(grad_k, axis=0, dtype=f32), tensor_at * kv_cols, 0
    )
    place_value = lax.dynamic_update_slice_in_dim(
        jnp.zeros_like(b_value), jnp.sum(grad_v, axis=0, dtype=f32), tensor_at * kv_cols, 0
    )
    sums = jnp.concatenate([gain_attn, gain_mlp, place_query, place_key, place_value])
    attn_terms = ctx_terms(scatter_whole(*after(attn_sums, pair_grads[1])))
    sums = after(sums, pair_grads[1]).reshape(-1, 128)
    sums = sum_everywhere(sums + swap_tensor(sums)).reshape(-1)
    splits = [model_width, 2 * model_width]
    splits += [splits[1] + b_query.shape[0], splits[1] + b_query.shape[0] + b_key.shape[0]]
    sum_attn, sum_mlp, sum_query, sum_key, sum_value = jnp.split(sums, splits)
    attn_grads = sum_terms(attn_terms)
    grad_w_qkv, grad_w_out = attn_grads[:, :-q_cols], attn_grads[:, -q_cols:]
    pair_grads = natural_ctx(pair_grads)
    grad_w_gate = hidden_grad(pair_grads[:, :, :ff_part], ff_cols)
    grad_w_up = hidden_grad(pair_grads[:, :, ff_part:], ff_cols)
    grad_w_query = grad_w_qkv[:, :q_cols]
    grad_w_key = grad_w_qkv[:, q_cols : q_cols + kv_cols]
    grad_w_value = grad_w_qkv[:, q_cols + kv_cols :]
    return (
        output,
        grad_tokens,
        grad_w_query,
        grad_w_key,
        grad_w_value,
        grad_w_out,
        grad_w_gate,
        grad_w_up,
        grad_w_down,
        sum_query,
        sum_key,
        sum_value,
        sum_attn,
        sum_mlp,
    )


def solution(mesh):
    placed = (
        P("dp", ("ctx", "tensor"), None),
        P("dp"),
        P(("dp", "ctx"), "tensor"),
        P(("dp", "ctx"), "tensor"),
        P(("dp", "ctx"), "tensor"),
        P(("dp", "ctx"), "tensor"),
        P(("dp", "ctx"), "tensor"),
        P(("dp", "ctx"), "tensor"),
        P(("dp", "ctx"), "tensor"),
        P(),
        P(),
        P(),
        P(),
        P(),
        P("dp", ("ctx", "tensor"), None),
    )
    return jax.shard_map(
        per_device,
        mesh=mesh,
        in_specs=placed,
        out_specs=(
            P("dp", ("ctx", "tensor"), None),
            P("dp", ("ctx", "tensor"), None),
            P(("dp", "ctx"), "tensor"),
            P(("dp", "ctx"), "tensor"),
            P(("dp", "ctx"), "tensor"),
            P(("dp", "ctx"), "tensor"),
            P(("dp", "ctx"), "tensor"),
            P(("dp", "ctx"), "tensor"),
            P(("dp", "ctx"), "tensor"),
            P(),
            P(),
            P(),
            P(),
            P(),
        ),
        check_vma=False,
    )
```
